256 devices in a mesh: grp: 4 (over x), blk: 64 (over z, y, core).
Axes of the slice: x: 4, y: 4, z: 8, core: 2. Of those that a mesh axis runs over, the one named last changes fastest.
Arguments:
- amplitudes: float32 [1600, 500, 256], P('blk', 'grp'), may hold values from -16 to 16
- cycle_weight: float32 [500, 20000], P(None, 'grp'), may hold values from -0.375 to 0.375
- occ_irrep: int32 [40], replicated, may hold values from 0 to 7
- vir_irrep: int32 [500], replicated, may hold values from 0 to 7
- occ_energy: float32 [40], replicated, may hold values from -1.5 to -0.4
- vir_energy: float32 [500], replicated, may hold values from 0.1 to 2.5
Outputs:
- increment: float32 [500, 10240], P('grp', 'blk')
The draws below stay inside these ranges and needn't reach their ends.
Inputs may be any that keep to these rules, and one draw needn't show every extreme that they name: `occ_irrep`: D2h irrep labels. `vir_irrep`: D2h irrep labels.
All inputs are finite; a program needn't handle non-finite values.
Results may differ from the reference program's by a relative error of at most 0.0001.
Values sent between devices are 32-bit elements; how exact they have to be, the bound alone decides.
No kernel may reach another device: no remote copies, remote signals or barrier semaphores. Data moves between devices by JAX's collectives and lax.ppermute only.
A program may use at most 128 MiB of HBM per device.

```python
import math
import jax
import jax.numpy as jnp
import numpy as np
from jax import lax

O = 40
V = 500
IW = 1
BW = 256


def with_ends(entries, key, low, largest):
    spot = [jax.random.randint(jax.random.fold_in(key, axis), (), 0, length) for axis, length in enumerate(entries.shape)]
    main_axis = entries.shape.index(max(entries.shape))
    next_to = spot[:main_axis] + [(spot[main_axis] + 1) % entries.shape[main_axis]] + spot[main_axis + 1:]
    return entries.at[tuple(spot)].set(low).at[tuple(next_to)].set(largest)


def raised(drawn, own_key, source, target, blocks, factor):
    def block_of(dim):
        return (jnp.arange(drawn.shape[dim]) // (drawn.shape[dim] // blocks)).reshape((-1,) + (1,) * (drawn.ndim - 1 - dim))

    one_side = jax.random.permutation(own_key, blocks)[block_of(target)]
    second = (block_of(target) + blocks // 2) % blocks
    return jnp.where((block_of(source) == one_side) | (block_of(source) == second), factor * drawn, drawn)


def steps_of(own_key, shape, split, least, top_value):
    level = 1.0
    for position, parts in split:
        draws = jax.random.uniform(jax.random.fold_in(jax.random.fold_in(own_key, 6), position), (parts,), jnp.float32, least / len(split), top_value / len(split))
        level = level * jnp.repeat(jnp.exp(draws), shape[position] // parts).reshape((-1,) + (1,) * (len(shape) - 1 - position))
    return level


def rank_bounds(number_of, skew):
    loads = [(1 << 20) // math.isqrt(grade ** skew) + 1 for grade in range(1, number_of + 1)]
    deviation = 1 + sum(loads) // (1 << 30)
    return np.cumsum(np.array([max(1, weight // deviation) for weight in loads]))


def ranked_ids(own_key, dims, amount, slope):
    table = rank_bounds(amount, slope)
    ticket = jax.random.randint(jax.random.fold_in(own_key, 1), dims, 0, int(table[amount - 1]))
    grade = jnp.searchsorted(jnp.asarray(table, jnp.int32), ticket, side="right")
    return jax.random.permutation(jax.random.fold_in(own_key, 2), amount)[grade].astype(jnp.int32)


def normal_values(stream_key, extent, width, reach, shards=(), dtype=jnp.bfloat16):
    factor_of = steps_of(stream_key, extent, shards, -0.22, 0.18) if shards else 1.0
    drawn = jax.random.normal(stream_key, extent, jnp.float32) * width * factor_of
    return jnp.minimum(jnp.maximum(drawn, -reach), reach).astype(dtype)


def bell_draw_with(stream_key, extent, deviation, most, pieces, heavy, dtype=jnp.bfloat16):
    drawn = deviation * jax.random.normal(stream_key, extent, jnp.float32)
    if pieces:
        drawn = drawn * steps_of(stream_key, extent, pieces, -0.22, 0.18)
    return jnp.clip(raised(drawn, jax.random.fold_in(stream_key, 3), *heavy), -most, most).astype(dtype)


def setup_inputs(seed: int = 0) -> dict:
    arg_keys = jax.random.split(jax.random.key(seed), 7)
    amplitudes = bell_draw_with(arg_keys[0], (O * O, V, BW), 1.0, 16.0, ((0, 64), (1, 4)), (0, 2, 64, 4.0), jnp.float32)
    cycle_weight = normal_values(arg_keys[1], (IW * V, V * O), (O * V // 72) ** -0.5, 0.375, ((1, 4),), jnp.float32)
    occ_irrep = with_ends(ranked_ids(arg_keys[2], (O,), 8, 1), jax.random.fold_in(arg_keys[2], 3), 0, 7).astype(jnp.int32)
    vir_irrep = with_ends(ranked_ids(arg_keys[3], (V,), 8, 1), jax.random.fold_in(arg_keys[3], 3), 0, 7).astype(jnp.int32)
    occ_energy = jnp.clip(jax.random.uniform(arg_keys[4], (O,), jnp.float32, -1.5, -0.4), -1.5, -0.4)
    vir_energy = jnp.clip(jax.random.uniform(arg_keys[5], (V,), jnp.float32, 0.1, 2.5), 0.1, 2.5)
    return {"amplitudes": amplitudes, "cycle_weight": cycle_weight, "occ_irrep": occ_irrep, "vir_irrep": vir_irrep, "occ_energy": occ_energy, "vir_energy": vir_energy}


def reference(amplitudes, cycle_weight, occ_irrep, vir_irrep, occ_energy, vir_energy):
    row_irrep = jnp.bitwise_xor(occ_irrep[:IW][:, None], vir_irrep[None, :]).reshape(IW * V)
    col_irrep = jnp.bitwise_xor(vir_irrep[:, None], occ_irrep[None, :]).reshape(V * O)
    weight = jnp.where(row_irrep[:, None] == col_irrep[None, :], cycle_weight, jnp.zeros_like(cycle_weight))
    weight = weight.reshape(IW * V, V, O)
    slab_irrep = vir_irrep[:BW]
    blocks = amplitudes.reshape(O, O, V, BW)

    def add_term(k, total):
        pair_irrep = jnp.bitwise_xor(lax.dynamic_index_in_dim(occ_irrep, k, 0, keepdims=False), occ_irrep)
        parity = jnp.bitwise_xor(jnp.bitwise_xor(pair_irrep[:, None, None], vir_irrep[None, :, None]), slab_irrep[None, None, :])
        block = lax.dynamic_index_in_dim(blocks, k, 0, keepdims=False)
        block = jnp.where(parity == 0, block, jnp.zeros_like(block))
        column = lax.dynamic_index_in_dim(weight, k, 2, keepdims=False)
        return total + jnp.einsum('xc,jcb->xbj', column, block, precision=lax.Precision.HIGHEST)

    total = lax.fori_loop(0, O, add_term, jnp.zeros((IW * V, BW, O), jnp.float32))
    row_energy = (occ_energy[:IW][:, None] - vir_energy[None, :]).reshape(IW * V)
    col_energy = occ_energy[None, :] - vir_energy[:BW][:, None]
    denominator = row_energy[:, None, None] + col_energy[None, :, :]
    return (total / denominator).reshape(IW * V, BW * O)
```

```python
import jax
import jax.numpy as jnp
from jax import lax
from jax.experimental import pallas as pl
from jax.experimental.pallas import tpu as pltpu
from jax.sharding import PartitionSpec as P

O = 40
V = 500
IW = 1
BW = 256
G = 4
M = 64
CL = V // G
CP = 128
T = O * O // M
TS = 5
BL = BW // M
J4 = O * BL
SLOTS = 640
FOLD = 40
NF = G * FOLD
NONE = 16

HIGHEST = lax.Precision.HIGHEST
F32 = jnp.float32
BF16 = jnp.bfloat16
I32 = jnp.int32


def dot(a, b):
    return jnp.dot(a, b, preferred_element_type=F32)


def halves(x):
    high = x.astype(BF16)
    return high, (x - high.astype(F32)).astype(BF16)


def iota(shape, dim):
    return lax.broadcasted_iota(I32, shape, dim)


def pack_kernel(occ_ref, vir_ref, amp_ref, out_ref, rank_ref, column_ref, count_ref, base_ref, total_ref, pick_ref, high_ref, low_ref):
    step = pl.program_id(0)
    g = lax.axis_index("grp")
    m = lax.axis_index("blk")
    row = vir_ref[:, 0:CP]
    for other in range(1, G):
        row = jnp.where(g == other, vir_ref[:, other * CL : other * CL + CP], row)
    row = jnp.where(iota((1, CP), 1) < CL, row, NONE)

    @pl.when(step == 0)
    def _():
        wide = jnp.broadcast_to(row, (CP, CP))
        column = jnp.transpose(wide)
        column_ref[...] = column
        before = (wide == column) & (iota((CP, CP), 0) < iota((CP, CP), 1))
        rank_ref[...] = jnp.sum(before.astype(F32), axis=0, keepdims=True).astype(I32)
        for q in range(8):
            same = (iota((8, CP), 0) == jnp.bitwise_xor(row, q)).astype(F32)
            count_ref[q] = jnp.broadcast_to(jnp.sum(same, axis=1, keepdims=True), (8, CP)).astype(I32)
        base_ref[...] = jnp.zeros_like(base_ref)
        total_ref[...] = jnp.zeros_like(total_ref)

    for t in range(TS):
        pair = m * T + step * TS + t
        q = jnp.bitwise_xor(occ_ref[pair // O], occ_ref[pair % O])
        same = iota((8, CP), 0) == jnp.bitwise_xor(row, q)
        base = jnp.sum(jnp.where(same, base_ref[...], 0).astype(F32), axis=0, keepdims=True).astype(I32)
        slot = base + rank_ref[...]
        base_ref[...] += count_ref[q]
        pick_ref[:, t * CP : (t + 1) * CP] = (iota((SLOTS, CP), 0) == slot).astype(F32).astype(BF16)
        need = jnp.bitwise_xor(column_ref[...], q)
        for half in range(BW // CP):
            lanes = slice(half * CP, (half + 1) * CP)
            block = jnp.where(need == vir_ref[:, lanes], amp_ref[t, :, lanes], 0.0)
            high, low = halves(block)
            high_ref[t * CP : (t + 1) * CP, lanes] = high
            low_ref[t * CP : (t + 1) * CP, lanes] = low
    total_ref[...] += dot(pick_ref[...], high_ref[...]) + dot(pick_ref[...], low_ref[...])

    @pl.when(step == pl.num_programs(0) - 1)
    def _():
        out_ref[...] = jnp.transpose(total_ref[...]).reshape(M, BL, SLOTS)


def pack(occ_irrep, vir_row, amplitudes):
    return pl.pallas_call(
        pack_kernel,
        name="pack_amplitudes",
        grid=(T // TS,),
        out_shape=jax.ShapeDtypeStruct((M, BL, SLOTS), F32),
        in_specs=[
            pl.BlockSpec(memory_space=pltpu.SMEM),
            pl.BlockSpec((1, G * CP), lambda s: (0, 0)),
            pl.BlockSpec((TS, CP, BW), lambda s: (s, 0, 0)),
        ],
        out_specs=pl.BlockSpec((M, BL, SLOTS), lambda s: (0, 0, 0)),
        scratch_shapes=[
            pltpu.VMEM((1, CP), I32),
            pltpu.VMEM((CP, CP), I32),
            pltpu.VMEM((8, 8, CP), I32),
            pltpu.VMEM((8, CP), I32),
            pltpu.VMEM((SLOTS, BW), F32),
            pltpu.VMEM((SLOTS, TS * CP), BF16),
            pltpu.VMEM((TS * CP, BW), BF16),
            pltpu.VMEM((TS * CP, BW), BF16),
        ],
        compiler_params=pltpu.CompilerParams(vmem_limit_bytes=32 << 20),
    )(occ_irrep, vir_row, amplitudes)


CS = 16


def fold_kernel(place_ref, need_ref, have_ref, w_ref, high_ref, low_ref, pick_ref, turn_ref, rest_ref):
    step = pl.program_id(0)

    @pl.when(step == 0)
    def _():
        pick_ref[...] = (iota((NF, V), 0) == place_ref[...]).astype(F32).astype(BF16)

    block = jnp.where(need_ref[...] == have_ref[...], w_ref[...], 0.0)
    high, low = halves(block)
    folded = dot(pick_ref[...], high) + dot(pick_ref[...], low)
    turned = jnp.transpose(folded)
    turn_ref[...] = turned[:, 0:CP]
    rest_ref[:, 0 : NF - CP] = turned[:, CP:NF]
    for k in range(O):
        rows = pl.ds(k, CS, stride=O)
        part = jnp.concatenate([turn_ref[rows, :], rest_ref[rows, :]], axis=1)
        high, low = halves(part[:, 0:NF])
        high_ref[k] = high
        low_ref[k] = low


def fold(place, need, have, weight):
    lanes = CS * O
    out = jax.ShapeDtypeStruct((O, CP, NF), BF16)
    spec = pl.BlockSpec((O, CS, NF), lambda s: (0, s, 0))
    return pl.pallas_call(
        fold_kernel,
        name="fold_weights",
        grid=(CP // CS,),
        out_shape=(out, out),
        in_specs=[
            pl.BlockSpec((1, V), lambda s: (0, 0)),
            pl.BlockSpec((V, 1), lambda s: (0, 0)),
            pl.BlockSpec((1, lanes), lambda s: (0, s)),
            pl.BlockSpec((V, lanes), lambda s: (0, s)),
        ],
        out_specs=(spec, spec),
        scratch_shapes=[pltpu.VMEM((NF, V), BF16), pltpu.VMEM((lanes, CP), F32), pltpu.VMEM((lanes, CP), F32)],
        compiler_params=pltpu.CompilerParams(vmem_limit_bytes=32 << 20),
    )(place, need, have, weight)


def contract_kernel(x_ref, slot_ref, high_ref, low_ref, out_ref, wide_ref, total_ref):
    g = lax.axis_index("grp")

    @pl.loop(0, M // 2)
    def _(i):
        packed = x_ref[pl.ds(2 * i, 2)].reshape(2 * BL, SLOTS)
        for t in range(T):
            slot = slot_ref[t, pl.ds(pl.multiple_of(8 * i, 8), 8), :]
            lane = jnp.bitwise_and(slot, CP - 1)
            where = jnp.right_shift(slot, 7)
            found = jnp.zeros((8, CP), F32)
            for part in range(SLOTS // CP):
                taken = jnp.take_along_axis(
                    packed[:, part * CP : (part + 1) * CP], lane, axis=1, mode="promise_in_bounds"
                )
                found = jnp.where(where == part, taken, found)
            first = pl.multiple_of(2 * T * BL * i, 8)
            wide_ref[pl.ds(first + BL * t, BL), :] = found[0:BL]
            wide_ref[pl.ds(first + T * BL + BL * t, BL), :] = found[BL : 2 * BL]

    total_ref[...] = jnp.zeros_like(total_ref)

    @pl.loop(0, O // 2)
    def _(i):
        first = pl.multiple_of(2 * J4 * i, 8)
        amp = jnp.concatenate([wide_ref[pl.ds(first, J4), :], wide_ref[pl.ds(first + J4, J4), :]], axis=1)
        a_high, a_low = halves(amp)
        w_high = high_ref[pl.ds(2 * i, 2)].reshape(2 * CP, NF)
        w_low = low_ref[pl.ds(2 * i, 2)].reshape(2 * CP, NF)
        total_ref[...] += dot(a_high, w_high) + dot(a_high, w_low) + dot(a_low, w_high)

    turned = jnp.transpose(total_ref[...])
    for block in range(G):
        out_ref[jnp.bitwise_xor(g, block)] = turned[block * FOLD : (block + 1) * FOLD]


def contract(received, slots, high, low):
    return pl.pallas_call(
        contract_kernel,
        name="contract",
        out_shape=jax.ShapeDtypeStruct((G, FOLD, J4), F32),
        scratch_shapes=[pltpu.VMEM((O * O * BL, CP), F32), pltpu.VMEM((J4, NF), F32)],
        compiler_params=pltpu.CompilerParams(vmem_limit_bytes=40 << 20),
    )(received, slots, high, low)


def finish_kernel(a_ref, b_ref, rank_ref, need_ref, have_ref, row_ref, column_ref, out_ref):
    folded = a_ref[...] + b_ref[...]
    source = iota((J4, J4), 0)
    target = iota((J4, J4), 1)
    move = (source % BL) * O + source // BL == target
    folded = jnp.dot(folded, move.astype(F32), precision=HIGHEST, preferred_element_type=F32)
    pick = (iota((CL, FOLD), 1) == rank_ref[...]).astype(F32)
    wide = jnp.dot(pick, folded, precision=HIGHEST, preferred_element_type=F32)
    wide = jnp.where(need_ref[...] == have_ref[...], wide, 0.0)
    out_ref[...] = wide / (row_ref[...] + column_ref[...])


def finish(a, b, rank, need, have, row, column):
    return pl.pallas_call(
        finish_kernel, name="finish", out_shape=jax.ShapeDtypeStruct((CL, J4), F32)
    )(a, b, rank, need, have, row, column)


def packed_form(amplitudes, cycle_weight, occ_irrep, vir_irrep, occ_energy, vir_energy):
    g = lax.axis_index("grp")
    m = lax.axis_index("blk")
    labels = jnp.arange(8, dtype=I32)
    sent = pack(occ_irrep, vir_irrep.reshape(1, V), amplitudes)
    received = lax.all_to_all(sent, "blk", 0, 0, tiled=True)

    shares = vir_irrep.reshape(G, CL)
    orbital = jnp.arange(CL)
    earlier = orbital[:, None] < orbital[None, :]
    ranks = jnp.sum((shares[:, :, None] == shares[:, None, :]) & earlier[None], axis=1).astype(I32)
    counts = jnp.sum(shares[:, :, None] == labels, axis=1).astype(I32)
    own = lax.dynamic_index_in_dim(shares, g, 0, keepdims=False)
    own_rank = lax.dynamic_index_in_dim(ranks, g, 0, keepdims=False)
    own_count = lax.dynamic_index_in_dim(counts, g, 0, keepdims=False)
    own_c = jnp.concatenate([own, jnp.full((CP - CL,), NONE, I32)])
    rank_c = jnp.concatenate([own_rank, jnp.zeros((CP - CL,), I32)])

    pairs = jnp.bitwise_xor(occ_irrep[:, None], occ_irrep[None, :]).reshape(M, T)
    kinds = (pairs[:, :, None] == labels).astype(I32)
    passed = jnp.cumsum(kinds, axis=1) - kinds
    crossed = jnp.bitwise_xor(labels[:, None], labels[None, :])
    per_kind = jnp.sum(jnp.where(crossed[:, :, None] == labels, own_count, 0), axis=2)
    base = jnp.sum(passed[:, :, :, None] * per_kind, axis=2)
    reach = jnp.bitwise_xor(pairs[:, :, None], own_c)
    slot = rank_c + sum(jnp.where(reach == u, base[:, :, u : u + 1], 0) for u in range(8))
    own_b = lax.dynamic_slice_in_dim(vir_irrep, m * BL, BL)
    slots = jnp.where(reach[:, :, None, :] == own_b[:, None], slot[:, :, None, :], -1)
    slots = jnp.transpose(slots, (1, 0, 2, 3)).reshape(T, M * BL, CP)

    totals = jnp.sum(kinds, axis=1)
    all_kinds = jnp.sum(jnp.where(crossed[:, :, None] == labels, counts[:, None, None, :], 0), axis=3)
    filled = jnp.sum(totals[None, :, :, None] * all_kinds[:, None], axis=2)
    fits = (jnp.max(filled) <= SLOTS) & (jnp.max(counts) <= FOLD)

    place = (jnp.minimum(ranks, FOLD) + jnp.where(ranks < FOLD, jnp.arange(G, dtype=I32)[:, None] * FOLD, V)).reshape(1, V)
    need = jnp.bitwise_xor(vir_irrep, occ_irrep[0]).reshape(V, 1)
    have = jnp.bitwise_xor(own_c[:, None], occ_irrep[None, :]).reshape(1, CP * O)
    high, low = fold(place, need, have, cycle_weight)

    partial = contract(received, slots, high, low)
    near = lax.ppermute(partial[1:3], "grp", [(d, d ^ 1) for d in range(G)])
    mine = partial[0] + near[0]
    last = lax.ppermute(partial[3] + near[1], "grp", [(d, d ^ 3) for d in range(G)])

    row_energy = occ_energy[0] - lax.dynamic_slice_in_dim(vir_energy, g * CL, CL)
    slab_energy = lax.dynamic_slice_in_dim(vir_energy, m * BL, BL)
    col_energy = (occ_energy[None, :] - slab_energy[:, None]).reshape(1, J4)
    row_need = jnp.bitwise_xor(own, occ_irrep[0]).reshape(CL, 1)
    col_have = jnp.bitwise_xor(occ_irrep[None, :], own_b[:, None]).reshape(1, J4)
    out = finish(mine, last, own_rank.reshape(CL, 1), row_need, col_have, row_energy.reshape(CL, 1), col_energy)
    return out, fits


def plain_form(amplitudes, cycle_weight, occ_irrep, vir_irrep, occ_energy, vir_energy):
    n_blk = lax.axis_size("blk")
    n_grp = lax.axis_size("grp")
    grp_index = lax.axis_index("grp")
    blk_index = lax.axis_index("blk")
    pair_loc, c_loc, slab = amplitudes.shape
    b_loc = slab // n_blk
    rows = IW * V
    out_rows = rows // n_grp
    vir_local = lax.dynamic_slice_in_dim(vir_irrep, grp_index * c_loc, c_loc)
    row_irrep = jnp.bitwise_xor(occ_irrep[:IW][:, None], vir_irrep[None, :]).reshape(rows)
    col_irrep = jnp.bitwise_xor(vir_local[:, None], occ_irrep[None, :])
    weight_all = cycle_weight.reshape(rows, c_loc, O)
    weight = jnp.where(
        row_irrep[:, None, None] == col_irrep[None, :, :], weight_all, jnp.zeros_like(weight_all)
    )
    row_energy = (occ_energy[:IW][:, None] - vir_energy[None, :]).reshape(rows)
    row_share = lax.dynamic_slice_in_dim(row_energy, grp_index * out_rows, out_rows)
    slab_energy = lax.dynamic_slice_in_dim(vir_energy, blk_index * b_loc, b_loc)
    col_energy = (occ_energy[None, :] - slab_energy[:, None]).reshape(b_loc * O)
    pair_index = blk_index * pair_loc + jnp.arange(pair_loc, dtype=jnp.int32)
    k_index = pair_index // O
    j_index = pair_index % O
    occ_ids = jnp.arange(O, dtype=jnp.int32)
    match_k = k_index[:, None] == occ_ids[None, :]
    match_j = j_index[:, None] == occ_ids[None, :]
    irrep_k = jnp.sum(jnp.where(match_k, occ_irrep[None, :], 0), axis=1)
    irrep_j = jnp.sum(jnp.where(match_j, occ_irrep[None, :], 0), axis=1)
    pair_irrep = jnp.bitwise_xor(irrep_k, irrep_j)
    parity = jnp.bitwise_xor(
        jnp.bitwise_xor(pair_irrep[:, None, None], vir_local[None, :, None]),
        vir_irrep[:slab][None, None, :],
    )
    masked = jnp.where(parity == 0, amplitudes, jnp.zeros_like(amplitudes))
    pick_k = match_k.astype(jnp.float32)
    pick_j = match_j.astype(jnp.float32)
    selected = jnp.einsum("xck,tk->xct", weight, pick_k, precision=HIGHEST)
    per_pair = jnp.einsum("xct,tcb->tbx", selected, masked, precision=HIGHEST)
    placed = jnp.einsum("tbx,tj->bjx", per_pair, pick_j, precision=HIGHEST)
    reduced = lax.psum_scatter(
        placed.reshape(b_loc * O * lax.axis_size("blk"), rows),
        "blk",
        scatter_dimension=0,
        tiled=True,
    )
    summed = jnp.transpose(lax.psum_scatter(reduced, "grp", scatter_dimension=1, tiled=True))
    denominator = row_share[:, None] + col_energy[None, :]
    return summed / denominator


def shards(*arrays):
    out, fits = packed_form(*arrays)
    return lax.cond(fits, lambda: out, lambda: plain_form(*arrays))


def solution(mesh):
    in_specs = (P("blk", "grp", None), P(None, "grp"), P(), P(), P(), P())
    out_specs = P("grp", "blk")
    return jax.shard_map(shards, mesh=mesh, in_specs=in_specs, out_specs=out_specs, check_vma=False)
```

```python
import jax
import jax.numpy as jnp
from jax import lax
from jax.experimental import pallas as pl
from jax.experimental.pallas import tpu as pltpu
from jax.sharding import PartitionSpec as P

O = 40
V = 500
IW = 1
BW = 256
G = 4
M = 64
CL = V // G
CP = 128
T = O * O // M
TS = 5
BL = BW // M
J4 = O * BL
SLOTS = 640
FOLD = 40
NF = G * FOLD
STEP_SLOTS = ((0, 176), (16, 304), (48, 416), (112, 528), (160, SLOTS))
PAIR_BLOCKS = ((0, 1),) * 3 + ((0, 2),) * 5 + ((0, 3),) * 5 + ((0, 4),) * 4 + ((1, 4),) * 2 + ((1, 5),) * 6
SLOT_FROM = tuple(max(CP * PAIR_BLOCKS[t][0], STEP_SLOTS[t // TS][0]) for t in range(T))
SLOT_TO = tuple(min(CP * PAIR_BLOCKS[t][1], STEP_SLOTS[t // TS][1]) for t in range(T))
NONE = 16

HIGHEST = lax.Precision.HIGHEST
F32 = jnp.float32
BF16 = jnp.bfloat16
I32 = jnp.int32


def dot(a, b):
    return jnp.dot(a, b, preferred_element_type=F32)


def halves(x):
    high = x.astype(BF16)
    return high, (x - high.astype(F32)).astype(BF16)


def iota(shape, dim):
    return lax.broadcasted_iota(I32, shape, dim)


def pack_kernel(occ_ref, vir_ref, amp_ref, out_ref, rank_ref, column_ref, count_ref, base_ref, total_ref, pick_ref, high_ref, low_ref):
    step = pl.program_id(0)
    g = lax.axis_index("grp")
    m = lax.axis_index("blk")
    row = vir_ref[:, 0:CP]
    for other in range(1, G):
        row = jnp.where(g == other, vir_ref[:, other * CL : other * CL + CP], row)
    row = jnp.where(iota((1, CP), 1) < CL, row, NONE)

    @pl.when(step == 0)
    def _():
        wide = jnp.broadcast_to(row, (CP, CP))
        column = jnp.transpose(wide)
        column_ref[...] = column
        before = (wide == column) & (iota((CP, CP), 0) < iota((CP, CP), 1))
        rank_ref[...] = jnp.sum(before.astype(F32), axis=0, keepdims=True).astype(I32)
        for q in range(8):
            same = (iota((8, CP), 0) == jnp.bitwise_xor(row, q)).astype(F32)
            count_ref[q] = jnp.broadcast_to(jnp.sum(same, axis=1, keepdims=True), (8, CP)).astype(I32)
        base_ref[...] = jnp.zeros_like(base_ref)
        total_ref[...] = jnp.zeros_like(total_ref)

    for phase, (first, last) in enumerate(STEP_SLOTS):

        @pl.when(step == phase)
        def _():
            for t in range(TS):
                pair = m * T + phase * TS + t
                q = jnp.bitwise_xor(occ_ref[pair // O], occ_ref[pair % O])
                same = iota((8, CP), 0) == jnp.bitwise_xor(row, q)
                base = jnp.sum(jnp.where(same, base_ref[...], 0).astype(F32), axis=0, keepdims=True).astype(I32)
                slot = base + rank_ref[...] - first
                base_ref[...] += count_ref[q]
                columns = slice(t * CP, (t + 1) * CP)
                pick_ref[0 : last - first, columns] = (iota((last - first, CP), 0) == slot).astype(F32).astype(BF16)
                need = jnp.bitwise_xor(column_ref[...], q)
                for half in range(BW // CP):
                    lanes = slice(half * CP, (half + 1) * CP)
                    block = jnp.where(need == vir_ref[:, lanes], amp_ref[t, :, lanes], 0.0)
                    high, low = halves(block)
                    high_ref[columns, lanes] = high
                    low_ref[columns, lanes] = low
            pick = pick_ref[0 : last - first]
            total_ref[first:last] += dot(pick, high_ref[...]) + dot(pick, low_ref[...])

    @pl.when(step == pl.num_programs(0) - 1)
    def _():
        out_ref[...] = jnp.transpose(total_ref[...]).reshape(M, BL, SLOTS)


def pack(occ_irrep, vir_row, amplitudes):
    return pl.pallas_call(
        pack_kernel,
        name="pack_amplitudes",
        grid=(T // TS,),
        out_shape=jax.ShapeDtypeStruct((M, BL, SLOTS), F32),
        in_specs=[
            pl.BlockSpec(memory_space=pltpu.SMEM),
            pl.BlockSpec((1, G * CP), lambda s: (0, 0)),
            pl.BlockSpec((TS, CP, BW), lambda s: (s, 0, 0)),
        ],
        out_specs=pl.BlockSpec((M, BL, SLOTS), lambda s: (0, 0, 0)),
        scratch_shapes=[
            pltpu.VMEM((1, CP), I32),
            pltpu.VMEM((CP, CP), I32),
            pltpu.VMEM((8, 8, CP), I32),
            pltpu.VMEM((8, CP), I32),
            pltpu.VMEM((SLOTS, BW), F32),
            pltpu.VMEM((SLOTS, TS * CP), BF16),
            pltpu.VMEM((TS * CP, BW), BF16),
            pltpu.VMEM((TS * CP, BW), BF16),
        ],
        compiler_params=pltpu.CompilerParams(vmem_limit_bytes=16 << 20),
    )(occ_irrep, vir_row, amplitudes)


CS = 16


def fold_kernel(place_ref, need_ref, have_ref, w_ref, high_ref, low_ref, pick_ref, turn_ref, rest_ref, first_ref, second_ref):
    step = pl.program_id(0)

    @pl.when(step == 0)
    def _():
        for first in range(0, V, CP):
            lanes = slice(first, min(first + CP, V))
            place = jnp.transpose(jnp.broadcast_to(place_ref[:, lanes], (CP, min(CP, V - first))))
            for at in range(0, NF, CP):
                wide = min(CP, NF - at)
                hit = iota((min(CP, V - first), wide), 1) + at == place[:, 0:wide]
                pick_ref[lanes, at : at + wide] = hit.astype(F32).astype(BF16)

    for part in range(CS * O // CP):
        rows = slice(part * CP, (part + 1) * CP)
        have = jnp.transpose(jnp.broadcast_to(have_ref[:, rows], (CP, CP)))
        for first in range(0, V, CP):
            lanes = slice(first, min(first + CP, V))
            kept = jnp.where(need_ref[:, lanes] == have[:, : min(CP, V - first)], w_ref[rows, lanes], 0.0)
            high, low = halves(kept)
            first_ref[rows, lanes] = high
            second_ref[rows, lanes] = low
    folded = dot(first_ref[...], pick_ref[...]) + dot(second_ref[...], pick_ref[...])
    turn_ref[...] = folded[:, 0:CP]
    rest_ref[:, 0 : NF - CP] = folded[:, CP:NF]
    for k in range(O):
        rows = pl.ds(k, CS, stride=O)
        part = jnp.concatenate([turn_ref[rows, :], rest_ref[rows, :]], axis=1)
        high, low = halves(part[:, 0:NF])
        high_ref[k] = high
        low_ref[k] = low


def fold(place, need, have, turned_weight):
    rows = CS * O
    out = jax.ShapeDtypeStruct((O, CP, NF), BF16)
    spec = pl.BlockSpec((O, CS, NF), lambda s: (0, s, 0))
    return pl.pallas_call(
        fold_kernel,
        name="fold_weights",
        grid=(CP // CS,),
        out_shape=(out, out),
        in_specs=[
            pl.BlockSpec((1, V), lambda s: (0, 0)),
            pl.BlockSpec((1, V), lambda s: (0, 0)),
            pl.BlockSpec((1, rows), lambda s: (0, s)),
            pl.BlockSpec((rows, V), lambda s: (s, 0)),
        ],
        out_specs=(spec, spec),
        scratch_shapes=[pltpu.VMEM((V, NF), BF16), pltpu.VMEM((rows, CP), F32), pltpu.VMEM((rows, CP), F32)]
        + [pltpu.VMEM((rows, V), BF16)] * 2,
        compiler_params=pltpu.CompilerParams(vmem_limit_bytes=16 << 20),
    )(place, need, have, turned_weight)


def contract_kernel(x_ref, slot_ref, far_high_ref, far_low_ref, out_ref, wide_ref, high_ref, low_ref, sem):
    g = lax.axis_index("grp")
    copies = [
        pltpu.make_async_copy(far_high_ref, high_ref, sem.at[0]),
        pltpu.make_async_copy(far_low_ref, low_ref, sem.at[1]),
    ]
    for copy in copies:
        copy.start()

    @pl.loop(0, M // 2)
    def _(i):
        packed = x_ref[pl.ds(2 * i, 2)].reshape(2 * BL, SLOTS)
        for t in range(T):
            slot = slot_ref[t, pl.ds(pl.multiple_of(8 * i, 8), 8), :]
            lane = jnp.bitwise_and(slot, CP - 1)
            where = jnp.right_shift(slot, 7)
            found = jnp.zeros((8, CP), F32)
            for part in range(*PAIR_BLOCKS[t]):
                taken = jnp.take_along_axis(
                    packed[:, part * CP : (part + 1) * CP], lane, axis=1, mode="promise_in_bounds"
                )
                found = jnp.where(where == part, taken, found)
            first = pl.multiple_of(2 * T * BL * i, 8)
            wide_ref[pl.ds(first + BL * t, BL), :] = found[0:BL]
            wide_ref[pl.ds(first + T * BL + BL * t, BL), :] = found[BL : 2 * BL]

    for copy in copies:
        copy.wait()
    total = jnp.zeros((J4, NF), F32)
    for i in range(O // 2):
        first = 2 * J4 * i
        amp = jnp.concatenate([wide_ref[first : first + J4], wide_ref[first + J4 : first + 2 * J4]], axis=1)
        a_high, a_low = halves(amp)
        w_high = high_ref[2 * i : 2 * i + 2].reshape(2 * CP, NF)
        w_low = low_ref[2 * i : 2 * i + 2].reshape(2 * CP, NF)
        total = total + (dot(a_high, w_high) + dot(a_high, w_low) + dot(a_low, w_high))

    turned = jnp.transpose(total)
    for block in range(G):
        out_ref[jnp.bitwise_xor(g, block)] = turned[block * FOLD : (block + 1) * FOLD]


def contract(received, slots, high, low):
    return pl.pallas_call(
        contract_kernel,
        name="contract",
        out_shape=jax.ShapeDtypeStruct((G, FOLD, J4), F32),
        in_specs=[
            pl.BlockSpec(memory_space=pltpu.VMEM),
            pl.BlockSpec(memory_space=pltpu.VMEM),
            pl.BlockSpec(memory_space=pl.ANY),
            pl.BlockSpec(memory_space=pl.ANY),
        ],
        scratch_shapes=[
            pltpu.VMEM((O * O * BL, CP), F32),
            pltpu.VMEM((O, CP, NF), BF16),
            pltpu.VMEM((O, CP, NF), BF16),
            pltpu.SemaphoreType.DMA((2,)),
        ],
        compiler_params=pltpu.CompilerParams(vmem_limit_bytes=24 << 20),
    )(received, slots, high, low)


def finish_kernel(a_ref, b_ref, rank_ref, need_ref, have_ref, row_ref, column_ref, out_ref):
    folded = a_ref[...] + b_ref[...]
    source = iota((J4, J4), 0)
    target = iota((J4, J4), 1)
    move = (source % BL) * O + source // BL == target
    folded = jnp.dot(folded, move.astype(F32), precision=HIGHEST, preferred_element_type=F32)
    pick = (iota((FOLD, CL), 0) == rank_ref[...]).astype(F32)
    wide = jnp.dot(jnp.transpose(folded), pick, precision=HIGHEST, preferred_element_type=F32)
    wide = jnp.where(need_ref[...] == have_ref[...], wide, 0.0)
    out_ref[...] = wide / (row_ref[...] + column_ref[...])


def finish(a, b, rank, need, have, row, column):
    return pl.pallas_call(
        finish_kernel,
        name="finish",
        out_shape=jax.ShapeDtypeStruct((J4, CL), F32),
        compiler_params=pltpu.CompilerParams(vmem_limit_bytes=4 << 20),
    )(a, b, rank, need, have, row, column)


def packed_form(amplitudes, cycle_weight, occ_irrep, vir_irrep, occ_energy, vir_energy):
    g = lax.axis_index("grp")
    m = lax.axis_index("blk")
    labels = jnp.arange(8, dtype=I32)
    sent = pack(occ_irrep, vir_irrep.reshape(1, V), amplitudes)
    received = lax.all_to_all(sent, "blk", 0, 0, tiled=True)

    shares = vir_irrep.reshape(G, CL)
    orbital = jnp.arange(CL)
    earlier = orbital[:, None] < orbital[None, :]
    ranks = jnp.sum((shares[:, :, None] == shares[:, None, :]) & earlier[None], axis=1).astype(I32)
    counts = jnp.sum(shares[:, :, None] == labels, axis=1).astype(I32)
    own = lax.dynamic_index_in_dim(shares, g, 0, keepdims=False)
    own_rank = lax.dynamic_index_in_dim(ranks, g, 0, keepdims=False)
    own_count = lax.dynamic_index_in_dim(counts, g, 0, keepdims=False)
    own_c = jnp.concatenate([own, jnp.full((CP - CL,), NONE, I32)])
    rank_c = jnp.concatenate([own_rank, jnp.zeros((CP - CL,), I32)])

    pairs = jnp.bitwise_xor(occ_irrep[:, None], occ_irrep[None, :]).reshape(M, T)
    kinds = (pairs[:, :, None] == labels).astype(I32)
    passed = jnp.cumsum(kinds, axis=1) - kinds
    crossed = jnp.bitwise_xor(labels[:, None], labels[None, :])
    per_kind = jnp.sum(jnp.where(crossed[:, :, None] == labels, own_count, 0), axis=2)
    base = jnp.sum(passed[:, :, :, None] * per_kind, axis=2)
    reach = jnp.bitwise_xor(pairs[:, :, None], own_c)
    slot = rank_c + sum(jnp.where(reach == u, base[:, :, u : u + 1], 0) for u in range(8))
    own_b = lax.dynamic_slice_in_dim(vir_irrep, m * BL, BL)
    slots = jnp.where(reach[:, :, None, :] == own_b[:, None], slot[:, :, None, :], -1)
    slots = jnp.transpose(slots, (1, 0, 2, 3)).reshape(T, M * BL, CP)

    all_kinds = jnp.sum(jnp.where(crossed[:, :, None] == labels, counts[:, None, None, :], 0), axis=3)
    before = jnp.sum(passed[None, :, :, :, None] * all_kinds[:, None, None], axis=3)
    least = jnp.min(before, axis=(0, 1, 3))
    most = jnp.max(before, axis=(0, 1, 3)) + jnp.max(counts)
    inside = (least >= jnp.array(SLOT_FROM)) & (most <= jnp.array(SLOT_TO))
    fits = jnp.all(inside) & (jnp.max(counts) <= FOLD)

    place = (jnp.minimum(ranks, FOLD) + jnp.where(ranks < FOLD, jnp.arange(G, dtype=I32)[:, None] * FOLD, V)).reshape(1, V)
    need = jnp.bitwise_xor(vir_irrep, occ_irrep[0]).reshape(1, V)
    have = jnp.bitwise_xor(own_c[:, None], occ_irrep[None, :]).reshape(1, CP * O)
    high, low = fold(place, need, have, cycle_weight.T)

    row_energy = (occ_energy[0] - lax.dynamic_slice_in_dim(vir_energy, g * CL, CL)).reshape(1, CL)
    slab_energy = lax.dynamic_slice_in_dim(vir_energy, m * BL, BL)
    col_energy = (occ_energy[None, :] - slab_energy[:, None]).reshape(J4, 1)
    row_need = jnp.bitwise_xor(own, occ_irrep[0]).reshape(1, CL)
    col_have = jnp.bitwise_xor(occ_irrep[None, :], own_b[:, None]).reshape(J4, 1)
    row_rank = own_rank.reshape(1, CL)
    slots, fits, row_rank, row_need, col_have, row_energy, col_energy = lax.optimization_barrier(
        (slots, fits, row_rank, row_need, col_have, row_energy, col_energy)
    )

    partial = contract(received, slots, high, low)
    near = lax.ppermute(partial[1:3], "grp", [(d, d ^ 1) for d in range(G)])
    mine = partial[0] + near[0]
    last = lax.ppermute(partial[3] + near[1], "grp", [(d, d ^ 3) for d in range(G)])
    out = finish(mine, last, row_rank, row_need, col_have, row_energy, col_energy)
    return out.T, fits


def plain_form(amplitudes, cycle_weight, occ_irrep, vir_irrep, occ_energy, vir_energy):
    g = lax.axis_index("grp")
    m = lax.axis_index("blk")
    own = lax.dynamic_slice_in_dim(vir_irrep, g * CL, CL)
    own_b = lax.dynamic_slice_in_dim(vir_irrep, m * BL, BL)
    sent = jnp.transpose(amplitudes.reshape(T * CL, BW)).reshape(M, BL, T * CL)
    received = lax.all_to_all(sent, "blk", 0, 0, tiled=True)
    amp = jnp.transpose(received.reshape(M, BL, T, CL), (0, 2, 1, 3)).reshape(O, O, BL, CL)
    pairs = jnp.bitwise_xor(occ_irrep[:, None], occ_irrep[None, :])
    allowed = jnp.bitwise_xor(pairs[:, :, None], own_b)[..., None] == own
    amp = jnp.where(allowed, amp, jnp.zeros_like(amp))
    weight = cycle_weight.reshape(V, CL, O)
    need = jnp.bitwise_xor(vir_irrep, occ_irrep[0])
    have = jnp.bitwise_xor(own[:, None], occ_irrep[None, :])
    weight = jnp.where(need[:, None, None] == have, weight, jnp.zeros_like(weight))
    partial = jnp.einsum("kjbc,xck->xbj", amp, weight, precision=HIGHEST).reshape(G, CL, J4)
    cycle = jnp.sum(lax.all_to_all(partial, "grp", 0, 0, tiled=True).reshape(G, CL, J4), axis=0)
    row_energy = occ_energy[0] - lax.dynamic_slice_in_dim(vir_energy, g * CL, CL)
    slab_energy = lax.dynamic_slice_in_dim(vir_energy, m * BL, BL)
    col_energy = (occ_energy[None, :] - slab_energy[:, None]).reshape(J4)
    return cycle / (row_energy[:, None] + col_energy[None, :])


def shards(*arrays):
    out, fits = packed_form(*arrays)
    return lax.cond(fits, lambda: out, lambda: plain_form(*arrays))


def solution(mesh):
    in_specs = (P("blk", "grp", None), P(None, "grp"), P(), P(), P(), P())
    out_specs = P("grp", "blk")
    return jax.shard_map(shards, mesh=mesh, in_specs=in_specs, out_specs=out_specs, check_vma=False)
```

```python
import jax
import jax.numpy as jnp
from jax import lax
from jax.experimental import pallas as pl
from jax.experimental.pallas import tpu as pltpu
from jax.sharding import PartitionSpec as P

O = 40
V = 500
IW = 1
BW = 256
G = 4
M = 64
CL = V // G
CP = 128
T = O * O // M
TS = 5
BL = BW // M
J4 = O * BL
SLOTS = 640
FOLD = 40
NF = G * FOLD
STEP_SLOTS = ((0, 176), (16, 304), (48, 416), (112, 528), (160, SLOTS))
PAIR_BLOCKS = ((0, 1),) * 3 + ((0, 2),) * 5 + ((0, 3),) * 5 + ((0, 4),) * 4 + ((1, 4),) * 2 + ((1, 5),) * 6
SLOT_FROM = tuple(max(CP * PAIR_BLOCKS[t][0], STEP_SLOTS[t // TS][0]) for t in range(T))
SLOT_TO = tuple(min(CP * PAIR_BLOCKS[t][1], STEP_SLOTS[t // TS][1]) for t in range(T))
NONE = 16

HIGHEST = lax.Precision.HIGHEST
F32 = jnp.float32
BF16 = jnp.bfloat16
I32 = jnp.int32


def dot(a, b):
    return jnp.dot(a, b, preferred_element_type=F32)


def halves(x):
    high = x.astype(BF16)
    return high, (x - high.astype(F32)).astype(BF16)


def in_hbm(x):
    return pltpu.with_memory_space_constraint(x, pltpu.HBM)


def iota(shape, dim):
    return lax.broadcasted_iota(I32, shape, dim)


def pack_kernel(occ_ref, vir_ref, amp_ref, out_ref, rank_ref, column_ref, count_ref, base_ref, total_ref, pick_ref, high_ref, low_ref):
    step = pl.program_id(0)
    g = lax.axis_index("grp")
    m = lax.axis_index("blk")
    row = vir_ref[:, 0:CP]
    for other in range(1, G):
        row = jnp.where(g == other, vir_ref[:, other * CL : other * CL + CP], row)
    row = jnp.where(iota((1, CP), 1) < CL, row, NONE)

    @pl.when(step == 0)
    def _():
        wide = jnp.broadcast_to(row, (CP, CP))
        column = jnp.transpose(wide)
        column_ref[...] = column
        before = (wide == column) & (iota((CP, CP), 0) < iota((CP, CP), 1))
        rank_ref[...] = jnp.sum(before.astype(F32), axis=0, keepdims=True).astype(I32)
        for q in range(8):
            same = (iota((8, CP), 0) == jnp.bitwise_xor(row, q)).astype(F32)
            count_ref[q] = jnp.broadcast_to(jnp.sum(same, axis=1, keepdims=True), (8, CP)).astype(I32)
        base_ref[...] = jnp.zeros_like(base_ref)
        total_ref[...] = jnp.zeros_like(total_ref)

    for phase, (first, last) in enumerate(STEP_SLOTS):

        @pl.when(step == phase)
        def _():
            for t in range(TS):
                pair = m * T + phase * TS + t
                q = jnp.bitwise_xor(occ_ref[pair // O], occ_ref[pair % O])
                same = iota((8, CP), 0) == jnp.bitwise_xor(row, q)
                base = jnp.sum(jnp.where(same, base_ref[...], 0).astype(F32), axis=0, keepdims=True).astype(I32)
                slot = base + rank_ref[...] - first
                base_ref[...] += count_ref[q]
                columns = slice(t * CP, (t + 1) * CP)
                pick_ref[0 : last - first, columns] = (iota((last - first, CP), 0) == slot).astype(F32).astype(BF16)
                need = jnp.bitwise_xor(column_ref[...], q)
                for half in range(BW // CP):
                    lanes = slice(half * CP, (half + 1) * CP)
                    block = jnp.where(need == vir_ref[:, lanes], amp_ref[t, :, lanes], 0.0)
                    high, low = halves(block)
                    high_ref[columns, lanes] = high
                    low_ref[columns, lanes] = low
            pick = pick_ref[0 : last - first]
            total_ref[first:last] += dot(pick, high_ref[...]) + dot(pick, low_ref[...])

    @pl.when(step == pl.num_programs(0) - 1)
    def _():
        out_ref[...] = jnp.transpose(total_ref[...]).reshape(M, BL, SLOTS)


def pack(occ_irrep, vir_row, amplitudes):
    return pl.pallas_call(
        pack_kernel,
        name="pack_amplitudes",
        grid=(T // TS,),
        out_shape=jax.ShapeDtypeStruct((M, BL, SLOTS), F32),
        in_specs=[
            pl.BlockSpec(memory_space=pltpu.SMEM),
            pl.BlockSpec((1, G * CP), lambda s: (0, 0)),
            pl.BlockSpec((TS, CP, BW), lambda s: (s, 0, 0)),
        ],
        out_specs=pl.BlockSpec((M, BL, SLOTS), lambda s: (0, 0, 0)),
        scratch_shapes=[
            pltpu.VMEM((1, CP), I32),
            pltpu.VMEM((CP, CP), I32),
            pltpu.VMEM((8, 8, CP), I32),
            pltpu.VMEM((8, CP), I32),
            pltpu.VMEM((SLOTS, BW), F32),
            pltpu.VMEM((SLOTS, TS * CP), BF16),
            pltpu.VMEM((TS * CP, BW), BF16),
            pltpu.VMEM((TS * CP, BW), BF16),
        ],
        compiler_params=pltpu.CompilerParams(vmem_limit_bytes=10 << 20),
    )(occ_irrep, vir_row, amplitudes)


CS = 16


def fold_kernel(place_ref, need_ref, have_ref, w_ref, high_ref, low_ref, pick_ref, turn_ref, rest_ref, first_ref, second_ref):
    step = pl.program_id(0)

    @pl.when(step == 0)
    def _():
        for first in range(0, V, CP):
            lanes = slice(first, min(first + CP, V))
            place = jnp.transpose(jnp.broadcast_to(place_ref[:, lanes], (CP, min(CP, V - first))))
            for at in range(0, NF, CP):
                wide = min(CP, NF - at)
                hit = iota((min(CP, V - first), wide), 1) + at == place[:, 0:wide]
                pick_ref[lanes, at : at + wide] = hit.astype(F32).astype(BF16)

    for part in range(CS * O // CP):
        rows = slice(part * CP, (part + 1) * CP)
        have = jnp.transpose(jnp.broadcast_to(have_ref[:, rows], (CP, CP)))
        for first in range(0, V, CP):
            lanes = slice(first, min(first + CP, V))
            kept = jnp.where(need_ref[:, lanes] == have[:, : min(CP, V - first)], w_ref[rows, lanes], 0.0)
            high, low = halves(kept)
            first_ref[rows, lanes] = high
            second_ref[rows, lanes] = low
    folded = dot(first_ref[...], pick_ref[...]) + dot(second_ref[...], pick_ref[...])
    turn_ref[...] = folded[:, 0:CP]
    rest_ref[:, 0 : NF - CP] = folded[:, CP:NF]
    for k in range(O):
        rows = pl.ds(k, CS, stride=O)
        part = jnp.concatenate([turn_ref[rows, :], rest_ref[rows, :]], axis=1)
        high, low = halves(part[:, 0:NF])
        high_ref[k] = high
        low_ref[k] = low


def fold(place, need, have, turned_weight):
    rows = CS * O
    out = pltpu.HBM((O, CP, NF), BF16)
    spec = pl.BlockSpec((O, CS, NF), lambda s: (0, s, 0))
    return pl.pallas_call(
        fold_kernel,
        name="fold_weights",
        grid=(CP // CS,),
        out_shape=(out, out),
        in_specs=[
            pl.BlockSpec((1, V), lambda s: (0, 0)),
            pl.BlockSpec((1, V), lambda s: (0, 0)),
            pl.BlockSpec((1, rows), lambda s: (0, s)),
            pl.BlockSpec((rows, V), lambda s: (s, 0)),
        ],
        out_specs=(spec, spec),
        scratch_shapes=[pltpu.VMEM((V, NF), BF16), pltpu.VMEM((rows, CP), F32), pltpu.VMEM((rows, CP), F32)]
        + [pltpu.VMEM((rows, V), BF16)] * 2,
        compiler_params=pltpu.CompilerParams(vmem_limit_bytes=10 << 20),
    )(place, need, have, turned_weight)


def contract_kernel(x_ref, slot_ref, far_high_ref, far_low_ref, out_ref, wide_ref, high_ref, low_ref, sem):
    g = lax.axis_index("grp")
    copies = [
        pltpu.make_async_copy(far_high_ref, high_ref, sem.at[0]),
        pltpu.make_async_copy(far_low_ref, low_ref, sem.at[1]),
    ]
    for copy in copies:
        copy.start()

    @pl.loop(0, M // 2)
    def _(i):
        packed = x_ref[pl.ds(2 * i, 2)].reshape(2 * BL, SLOTS)
        for t in range(T):
            slot = slot_ref[t, pl.ds(pl.multiple_of(8 * i, 8), 8), :]
            lane = jnp.bitwise_and(slot, CP - 1)
            where = jnp.right_shift(slot, 7)
            found = jnp.zeros((8, CP), F32)
            for part in range(*PAIR_BLOCKS[t]):
                taken = jnp.take_along_axis(
                    packed[:, part * CP : (part + 1) * CP], lane, axis=1, mode="promise_in_bounds"
                )
                found = jnp.where(where == part, taken, found)
            first = pl.multiple_of(2 * T * BL * i, 8)
            wide_ref[pl.ds(first + BL * t, BL), :] = found[0:BL]
            wide_ref[pl.ds(first + T * BL + BL * t, BL), :] = found[BL : 2 * BL]

    for copy in copies:
        copy.wait()
    total = jnp.zeros((J4, NF), F32)
    for i in range(O // 2):
        first = 2 * J4 * i
        amp = jnp.concatenate([wide_ref[first : first + J4], wide_ref[first + J4 : first + 2 * J4]], axis=1)
        a_high, a_low = halves(amp)
        w_high = high_ref[2 * i : 2 * i + 2].reshape(2 * CP, NF)
        w_low = low_ref[2 * i : 2 * i + 2].reshape(2 * CP, NF)
        total = total + (dot(a_high, w_high) + dot(a_high, w_low) + dot(a_low, w_high))

    turned = jnp.transpose(total)
    for block in range(G):
        out_ref[jnp.bitwise_xor(g, block)] = turned[block * FOLD : (block + 1) * FOLD]


def contract(received, slots, high, low):
    return pl.pallas_call(
        contract_kernel,
        name="contract",
        out_shape=jax.ShapeDtypeStruct((G, FOLD, J4), F32),
        in_specs=[
            pl.BlockSpec(memory_space=pltpu.VMEM),
            pl.BlockSpec(memory_space=pltpu.VMEM),
            pl.BlockSpec(memory_space=pltpu.HBM),
            pl.BlockSpec(memory_space=pltpu.HBM),
        ],
        scratch_shapes=[
            pltpu.VMEM((O * O * BL, CP), F32),
            pltpu.VMEM((O, CP, NF), BF16),
            pltpu.VMEM((O, CP, NF), BF16),
            pltpu.SemaphoreType.DMA((2,)),
        ],
        compiler_params=pltpu.CompilerParams(vmem_limit_bytes=14 << 20),
    )(received, slots, in_hbm(high), in_hbm(low))


def finish_kernel(a_ref, b_ref, rank_ref, need_ref, have_ref, row_ref, column_ref, out_ref):
    folded = a_ref[...] + b_ref[...]
    source = iota((J4, J4), 0)
    target = iota((J4, J4), 1)
    move = (source % BL) * O + source // BL == target
    folded = jnp.dot(folded, move.astype(F32), precision=HIGHEST, preferred_element_type=F32)
    pick = (iota((FOLD, CL), 0) == rank_ref[...]).astype(F32)
    wide = jnp.dot(jnp.transpose(folded), pick, precision=HIGHEST, preferred_element_type=F32)
    wide = jnp.where(need_ref[...] == have_ref[...], wide, 0.0)
    out_ref[...] = wide / (row_ref[...] + column_ref[...])


def finish(a, b, rank, need, have, row, column):
    return pl.pallas_call(
        finish_kernel,
        name="finish",
        out_shape=pltpu.HBM((J4, CL), F32),
        compiler_params=pltpu.CompilerParams(vmem_limit_bytes=4 << 20),
    )(a, b, rank, need, have, row, column)


def packed_form(amplitudes, cycle_weight, occ_irrep, vir_irrep, occ_energy, vir_energy):
    g = lax.axis_index("grp")
    m = lax.axis_index("blk")
    labels = jnp.arange(8, dtype=I32)
    sent = pack(occ_irrep, vir_irrep.reshape(1, V), amplitudes)
    received = lax.all_to_all(sent, "blk", 0, 0, tiled=True)

    shares = vir_irrep.reshape(G, CL)
    orbital = jnp.arange(CL)
    earlier = orbital[:, None] < orbital[None, :]
    ranks = jnp.sum((shares[:, :, None] == shares[:, None, :]) & earlier[None], axis=1).astype(I32)
    counts = jnp.sum(shares[:, :, None] == labels, axis=1).astype(I32)
    own = lax.dynamic_index_in_dim(shares, g, 0, keepdims=False)
    own_rank = lax.dynamic_index_in_dim(ranks, g, 0, keepdims=False)
    own_count = lax.dynamic_index_in_dim(counts, g, 0, keepdims=False)
    own_c = jnp.concatenate([own, jnp.full((CP - CL,), NONE, I32)])
    rank_c = jnp.concatenate([own_rank, jnp.zeros((CP - CL,), I32)])

    pairs = jnp.bitwise_xor(occ_irrep[:, None], occ_irrep[None, :]).reshape(M, T)
    kinds = (pairs[:, :, None] == labels).astype(I32)
    passed = jnp.cumsum(kinds, axis=1) - kinds
    crossed = jnp.bitwise_xor(labels[:, None], labels[None, :])
    per_kind = jnp.sum(jnp.where(crossed[:, :, None] == labels, own_count, 0), axis=2)
    base = jnp.sum(passed[:, :, :, None] * per_kind, axis=2)
    reach = jnp.bitwise_xor(pairs[:, :, None], own_c)
    slot = rank_c + sum(jnp.where(reach == u, base[:, :, u : u + 1], 0) for u in range(8))
    own_b = lax.dynamic_slice_in_dim(vir_irrep, m * BL, BL)
    slots = jnp.where(reach[:, :, None, :] == own_b[:, None], slot[:, :, None, :], -1)
    slots = jnp.transpose(slots, (1, 0, 2, 3)).reshape(T, M * BL, CP)

    all_kinds = jnp.sum(jnp.where(crossed[:, :, None] == labels, counts[:, None, None, :], 0), axis=3)
    before = jnp.sum(passed[None, :, :, :, None] * all_kinds[:, None, None], axis=3)
    least = jnp.min(before, axis=(0, 1, 3))
    most = jnp.max(before, axis=(0, 1, 3)) + jnp.max(counts)
    inside = (least >= jnp.array(SLOT_FROM)) & (most <= jnp.array(SLOT_TO))
    fits = jnp.all(inside) & (jnp.max(counts) <= FOLD)

    place = (jnp.minimum(ranks, FOLD) + jnp.where(ranks < FOLD, jnp.arange(G, dtype=I32)[:, None] * FOLD, V)).reshape(1, V)
    need = jnp.bitwise_xor(vir_irrep, occ_irrep[0]).reshape(1, V)
    have = jnp.bitwise_xor(own_c[:, None], occ_irrep[None, :]).reshape(1, CP * O)
    high, low = fold(place, need, have, cycle_weight.T)

    row_energy = (occ_energy[0] - lax.dynamic_slice_in_dim(vir_energy, g * CL, CL)).reshape(1, CL)
    slab_energy = lax.dynamic_slice_in_dim(vir_energy, m * BL, BL)
    col_energy = (occ_energy[None, :] - slab_energy[:, None]).reshape(J4, 1)
    row_need = jnp.bitwise_xor(own, occ_irrep[0]).reshape(1, CL)
    col_have = jnp.bitwise_xor(occ_irrep[None, :], own_b[:, None]).reshape(J4, 1)
    row_rank = own_rank.reshape(1, CL)
    slots, fits, row_rank, row_need, col_have, row_energy, col_energy = lax.optimization_barrier(
        (slots, fits, row_rank, row_need, col_have, row_energy, col_energy)
    )

    partial = contract(received, slots, high, low)
    near = lax.ppermute(partial[1:3], "grp", [(d, d ^ 1) for d in range(G)])
    mine = partial[0] + near[0]
    last = lax.ppermute(partial[3] + near[1], "grp", [(d, d ^ 3) for d in range(G)])
    out = finish(mine, last, row_rank, row_need, col_have, row_energy, col_energy)
    return out.T, fits


def plain_form(amplitudes, cycle_weight, occ_irrep, vir_irrep, occ_energy, vir_energy):
    g = lax.axis_index("grp")
    m = lax.axis_index("blk")
    own = lax.dynamic_slice_in_dim(vir_irrep, g * CL, CL)
    own_b = lax.dynamic_slice_in_dim(vir_irrep, m * BL, BL)
    sent = jnp.transpose(amplitudes.reshape(T * CL, BW)).reshape(M, BL, T * CL)
    received = lax.all_to_all(sent, "blk", 0, 0, tiled=True)
    amp = jnp.transpose(received.reshape(M, BL, T, CL), (0, 2, 1, 3)).reshape(O, O, BL, CL)
    pairs = jnp.bitwise_xor(occ_irrep[:, None], occ_irrep[None, :])
    allowed = jnp.bitwise_xor(pairs[:, :, None], own_b)[..., None] == own
    amp = jnp.where(allowed, amp, jnp.zeros_like(amp))
    weight = cycle_weight.reshape(V, CL, O)
    need = jnp.bitwise_xor(vir_irrep, occ_irrep[0])
    have = jnp.bitwise_xor(own[:, None], occ_irrep[None, :])
    weight = jnp.where(need[:, None, None] == have, weight, jnp.zeros_like(weight))
    partial = jnp.einsum("kjbc,xck->xbj", amp, weight, precision=HIGHEST).reshape(G, CL, J4)
    cycle = jnp.sum(lax.all_to_all(partial, "grp", 0, 0, tiled=True).reshape(G, CL, J4), axis=0)
    row_energy = occ_energy[0] - lax.dynamic_slice_in_dim(vir_energy, g * CL, CL)
    slab_energy = lax.dynamic_slice_in_dim(vir_energy, m * BL, BL)
    col_energy = (occ_energy[None, :] - slab_energy[:, None]).reshape(J4)
    return cycle / (row_energy[:, None] + col_energy[None, :])


def shards(*arrays):
    out, fits = packed_form(*arrays)
    return lax.cond(fits, lambda: out, lambda: plain_form(*arrays))


def solution(mesh):
    in_specs = (P("blk", "grp", None), P(None, "grp"), P(), P(), P(), P())
    out_specs = P("grp", "blk")
    return jax.shard_map(shards, mesh=mesh, in_specs=in_specs, out_specs=out_specs, check_vma=False)
```

```python
import jax
import jax.numpy as jnp
from jax import lax
from jax.experimental import pallas as pl
from jax.experimental.pallas import tpu as pltpu
from jax.sharding import PartitionSpec as P

O = 40
V = 500
IW = 1
BW = 256
G = 4
M = 64
CL = V // G
CP = 128
T = O * O // M
TS = 5
BL = BW // M
J4 = O * BL
SLOTS = 640
FOLD = 40
NF = G * FOLD
GT = 3
NG = -(-T // GT)
STEP_SLOTS = ((0, 176), (16, 304), (48, 416), (112, 528), (160, SLOTS))
GROUP_BLOCKS = ((0, 1), (0, 2), (0, 3), (0, 3), (0, 4), (0, 4), (1, 5), (1, 5), (1, 5))
SLOT_FROM = tuple(max(CP * GROUP_BLOCKS[t // GT][0], STEP_SLOTS[t // TS][0]) for t in range(T))
SLOT_TO = tuple(min(CP * GROUP_BLOCKS[t // GT][1], STEP_SLOTS[t // TS][1]) for t in range(T))
NONE = 16

HIGHEST = lax.Precision.HIGHEST
F32 = jnp.float32
BF16 = jnp.bfloat16
I32 = jnp.int32


def dot(a, b):
    return jnp.dot(a, b, preferred_element_type=F32)


def halves(x):
    high = x.astype(BF16)
    return high, (x - high.astype(F32)).astype(BF16)


def in_hbm(x):
    return pltpu.with_memory_space_constraint(x, pltpu.HBM)


def iota(shape, dim):
    return lax.broadcasted_iota(I32, shape, dim)


def pack_kernel(occ_ref, vir_ref, amp_ref, out_ref, rank_ref, column_ref, count_ref, base_ref, total_ref, pick_ref, high_ref, low_ref):
    step = pl.program_id(0)
    g = lax.axis_index("grp")
    m = lax.axis_index("blk")
    row = vir_ref[:, 0:CP]
    for other in range(1, G):
        row = jnp.where(g == other, vir_ref[:, other * CL : other * CL + CP], row)
    row = jnp.where(iota((1, CP), 1) < CL, row, NONE)

    @pl.when(step == 0)
    def _():
        wide = jnp.broadcast_to(row, (CP, CP))
        column = jnp.transpose(wide)
        column_ref[...] = column
        before = (wide == column) & (iota((CP, CP), 0) < iota((CP, CP), 1))
        rank_ref[...] = jnp.sum(before.astype(F32), axis=0, keepdims=True).astype(I32)
        for q in range(8):
            same = (iota((8, CP), 0) == jnp.bitwise_xor(row, q)).astype(F32)
            count_ref[q] = jnp.broadcast_to(jnp.sum(same, axis=1, keepdims=True), (8, CP)).astype(I32)
        base_ref[...] = jnp.zeros_like(base_ref)
        total_ref[...] = jnp.zeros_like(total_ref)

    for phase, (first, last) in enumerate(STEP_SLOTS):

        @pl.when(step == phase)
        def _():
            for t in range(TS):
                pair = m * T + phase * TS + t
                q = jnp.bitwise_xor(occ_ref[pair // O], occ_ref[pair % O])
                same = iota((8, CP), 0) == jnp.bitwise_xor(row, q)
                base = jnp.sum(jnp.where(same, base_ref[...], 0).astype(F32), axis=0, keepdims=True).astype(I32)
                slot = base + rank_ref[...] - first
                base_ref[...] += count_ref[q]
                columns = slice(t * CP, (t + 1) * CP)
                pick_ref[0 : last - first, columns] = (iota((last - first, CP), 0) == slot).astype(F32).astype(BF16)
                need = jnp.bitwise_xor(column_ref[...], q)
                for half in range(BW // CP):
                    lanes = slice(half * CP, (half + 1) * CP)
                    block = jnp.where(need == vir_ref[:, lanes], amp_ref[t, :, lanes], 0.0)
                    high, low = halves(block)
                    high_ref[columns, lanes] = high
                    low_ref[columns, lanes] = low
            pick = pick_ref[0 : last - first]
            total_ref[first:last] += dot(pick, high_ref[...]) + dot(pick, low_ref[...])

    @pl.when(step == pl.num_programs(0) - 1)
    def _():
        out_ref[...] = jnp.transpose(total_ref[...]).reshape(M, BL, SLOTS)


def pack(occ_irrep, vir_row, amplitudes):
    return pl.pallas_call(
        pack_kernel,
        name="pack_amplitudes",
        grid=(T // TS,),
        out_shape=jax.ShapeDtypeStruct((M, BL, SLOTS), F32),
        in_specs=[
            pl.BlockSpec(memory_space=pltpu.SMEM),
            pl.BlockSpec((1, G * CP), lambda s: (0, 0)),
            pl.BlockSpec((TS, CP, BW), lambda s: (s, 0, 0)),
        ],
        out_specs=pl.BlockSpec((M, BL, SLOTS), lambda s: (0, 0, 0)),
        scratch_shapes=[
            pltpu.VMEM((1, CP), I32),
            pltpu.VMEM((CP, CP), I32),
            pltpu.VMEM((8, 8, CP), I32),
            pltpu.VMEM((8, CP), I32),
            pltpu.VMEM((SLOTS, BW), F32),
            pltpu.VMEM((SLOTS, TS * CP), BF16),
            pltpu.VMEM((TS * CP, BW), BF16),
            pltpu.VMEM((TS * CP, BW), BF16),
        ],
        compiler_params=pltpu.CompilerParams(vmem_limit_bytes=8 << 20),
    )(occ_irrep, vir_row, amplitudes)


CS = 16


def fold_kernel(place_ref, need_ref, have_ref, w_ref, high_ref, low_ref, pick_ref, turn_ref, rest_ref, first_ref, second_ref):
    step = pl.program_id(0)

    @pl.when(step == 0)
    def _():
        for first in range(0, V, CP):
            lanes = slice(first, min(first + CP, V))
            place = jnp.transpose(jnp.broadcast_to(place_ref[:, lanes], (CP, min(CP, V - first))))
            for at in range(0, NF, CP):
                wide = min(CP, NF - at)
                hit = iota((min(CP, V - first), wide), 1) + at == place[:, 0:wide]
                pick_ref[lanes, at : at + wide] = hit.astype(F32).astype(BF16)

    for part in range(CS * O // CP):
        rows = slice(part * CP, (part + 1) * CP)
        have = jnp.transpose(jnp.broadcast_to(have_ref[:, rows], (CP, CP)))
        for first in range(0, V, CP):
            lanes = slice(first, min(first + CP, V))
            kept = jnp.where(need_ref[:, lanes] == have[:, : min(CP, V - first)], w_ref[rows, lanes], 0.0)
            high, low = halves(kept)
            first_ref[rows, lanes] = high
            second_ref[rows, lanes] = low
    folded = dot(first_ref[...], pick_ref[...]) + dot(second_ref[...], pick_ref[...])
    turn_ref[...] = folded[:, 0:CP]
    rest_ref[:, 0 : NF - CP] = folded[:, CP:NF]
    for k in range(O):
        rows = pl.ds(k, CS, stride=O)
        part = jnp.concatenate([turn_ref[rows, :], rest_ref[rows, :]], axis=1)
        high, low = halves(part[:, 0:NF])
        high_ref[k] = high
        low_ref[k] = low


def fold(place, need, have, turned_weight):
    rows = CS * O
    out = pltpu.HBM((O, CP, NF), BF16)
    spec = pl.BlockSpec((O, CS, NF), lambda s: (0, s, 0))
    return pl.pallas_call(
        fold_kernel,
        name="fold_weights",
        grid=(CP // CS,),
        out_shape=(out, out),
        in_specs=[
            pl.BlockSpec((1, V), lambda s: (0, 0)),
            pl.BlockSpec((1, V), lambda s: (0, 0)),
            pl.BlockSpec((1, rows), lambda s: (0, s)),
            pl.BlockSpec((rows, V), lambda s: (s, 0)),
        ],
        out_specs=(spec, spec),
        scratch_shapes=[pltpu.VMEM((V, NF), BF16), pltpu.VMEM((rows, CP), F32), pltpu.VMEM((rows, CP), F32)]
        + [pltpu.VMEM((rows, V), BF16)] * 2,
        compiler_params=pltpu.CompilerParams(vmem_limit_bytes=8 << 20),
    )(place, need, have, turned_weight)


def contract_kernel(
    x_ref, slot_ref, valid_ref, rank_ref, far_high_ref, far_low_ref, out_ref, seen_ref, spread_ref, wide_ref, high_ref, low_ref, sem
):
    g = lax.axis_index("grp")
    copies = [
        pltpu.make_async_copy(far_high_ref, high_ref, sem.at[0]),
        pltpu.make_async_copy(far_low_ref, low_ref, sem.at[1]),
    ]
    for copy in copies:
        copy.start()

    @pl.loop(0, M // 2)
    def _(i):
        packed = x_ref[pl.ds(2 * i, 2)].reshape(2 * BL, SLOTS)
        rows = pl.ds(pl.multiple_of(8 * i, 8), 8)
        for group, (first, last) in enumerate(GROUP_BLOCKS):
            slot = slot_ref[group, rows, :]
            lane = jnp.bitwise_and(slot, CP - 1)
            where = jnp.right_shift(slot, 7)
            found = jnp.zeros((8, CP), F32)
            for part in range(first, last):
                taken = jnp.take_along_axis(
                    packed[:, part * CP : (part + 1) * CP], lane, axis=1, mode="promise_in_bounds"
                )
                found = jnp.where(where == part, taken, found)
            seen_ref[group, rows, :] = found

    place = [(iota((CP, CP), 0) - at * FOLD == rank_ref[...]).astype(F32).astype(BF16) for at in range(GT)]
    place = jnp.concatenate(place, axis=1)
    place = jnp.concatenate([place, place], axis=0)
    for group in range(NG):
        spread_ref[group] = dot(jnp.concatenate(halves(seen_ref[group]), axis=1), place)

    @pl.loop(0, M // 2)
    def _(i):
        rows = pl.ds(pl.multiple_of(8 * i, 8), 8)
        first = pl.multiple_of(2 * T * BL * i, 8)
        for t in range(T):
            at = (t % GT) * CP
            row = spread_ref[t // GT, rows, at : at + CP] * valid_ref[t, rows, :]
            if t % 2 == 0:
                one, two = row[0:BL], row[BL : 2 * BL]
            else:
                row = pltpu.roll(row, BL, 0)
                one, two = row[BL : 2 * BL], row[0:BL]
            wide_ref[pl.ds(first + BL * t, BL), :] = one
            wide_ref[pl.ds(first + T * BL + BL * t, BL), :] = two

    for copy in copies:
        copy.wait()
    total = jnp.zeros((J4, NF), F32)
    for i in range(O // 2):
        first = 2 * J4 * i
        amp = jnp.concatenate([wide_ref[first : first + J4], wide_ref[first + J4 : first + 2 * J4]], axis=1)
        a_high, a_low = halves(amp)
        w_high = high_ref[2 * i : 2 * i + 2].reshape(2 * CP, NF)
        w_low = low_ref[2 * i : 2 * i + 2].reshape(2 * CP, NF)
        total = total + (dot(a_high, w_high) + dot(a_high, w_low) + dot(a_low, w_high))

    turned = jnp.transpose(total)
    for block in range(G):
        out_ref[jnp.bitwise_xor(g, block)] = turned[block * FOLD : (block + 1) * FOLD]


def contract(received, slots, valid, rank, high, low):
    vmem = pl.BlockSpec(memory_space=pltpu.VMEM)
    return pl.pallas_call(
        contract_kernel,
        name="contract",
        out_shape=jax.ShapeDtypeStruct((G, FOLD, J4), F32),
        in_specs=[vmem] * 4 + [pl.BlockSpec(memory_space=pltpu.HBM)] * 2,
        scratch_shapes=[
            pltpu.VMEM((NG, M * BL, CP), F32),
            pltpu.VMEM((NG, M * BL, GT * CP), F32),
            pltpu.VMEM((O * O * BL, CP), F32),
            pltpu.VMEM((O, CP, NF), BF16),
            pltpu.VMEM((O, CP, NF), BF16),
            pltpu.SemaphoreType.DMA((2,)),
        ],
        compiler_params=pltpu.CompilerParams(vmem_limit_bytes=16 << 20),
    )(received, slots, valid, rank, in_hbm(high), in_hbm(low))


def finish_kernel(a_ref, b_ref, rank_ref, need_ref, have_ref, row_ref, column_ref, out_ref):
    folded = a_ref[...] + b_ref[...]
    source = iota((J4, J4), 0)
    target = iota((J4, J4), 1)
    move = (source % BL) * O + source // BL == target
    folded = jnp.dot(folded, move.astype(F32), precision=HIGHEST, preferred_element_type=F32)
    pick = (iota((FOLD, CL), 0) == rank_ref[...]).astype(F32)
    wide = jnp.dot(jnp.transpose(folded), pick, precision=HIGHEST, preferred_element_type=F32)
    wide = jnp.where(need_ref[...] == have_ref[...], wide, 0.0)
    out_ref[...] = wide / (row_ref[...] + column_ref[...])


def finish(a, b, rank, need, have, row, column):
    return pl.pallas_call(
        finish_kernel,
        name="finish",
        out_shape=pltpu.HBM((J4, CL), F32),
        compiler_params=pltpu.CompilerParams(vmem_limit_bytes=4 << 20),
    )(a, b, rank, need, have, row, column)


def packed_form(amplitudes, cycle_weight, occ_irrep, vir_irrep, occ_energy, vir_energy):
    g = lax.axis_index("grp")
    m = lax.axis_index("blk")
    labels = jnp.arange(8, dtype=I32)
    sent = pack(occ_irrep, vir_irrep.reshape(1, V), amplitudes)
    received = lax.all_to_all(sent, "blk", 0, 0, tiled=True)

    shares = vir_irrep.reshape(G, CL)
    orbital = jnp.arange(CL)
    earlier = orbital[:, None] < orbital[None, :]
    ranks = jnp.sum((shares[:, :, None] == shares[:, None, :]) & earlier[None], axis=1).astype(I32)
    counts = jnp.sum(shares[:, :, None] == labels, axis=1).astype(I32)
    own = lax.dynamic_index_in_dim(shares, g, 0, keepdims=False)
    own_rank = lax.dynamic_index_in_dim(ranks, g, 0, keepdims=False)
    own_count = lax.dynamic_index_in_dim(counts, g, 0, keepdims=False)
    own_c = jnp.concatenate([own, jnp.full((CP - CL,), NONE, I32)])
    rank_c = jnp.concatenate([own_rank, jnp.zeros((CP - CL,), I32)])

    pairs = jnp.bitwise_xor(occ_irrep[:, None], occ_irrep[None, :]).reshape(M, T)
    kinds = (pairs[:, :, None] == labels).astype(I32)
    passed = jnp.cumsum(kinds, axis=1) - kinds
    crossed = jnp.bitwise_xor(labels[:, None], labels[None, :])
    own_b = lax.dynamic_slice_in_dim(vir_irrep, m * BL, BL)
    per_b = jnp.sum(jnp.where(jnp.bitwise_xor(labels[:, None], own_b)[:, :, None] == labels, own_count, 0), axis=2)
    start = jnp.sum(passed[:, :, None, :] * per_b.T, axis=3)
    amount = jnp.sum(kinds[:, :, None, :] * per_b.T, axis=3)

    def by_group(x):
        x = jnp.pad(jnp.transpose(x, (1, 0, 2)), ((0, NG * GT - T), (0, 0), (0, 0)))
        return x.reshape(NG, GT, M * BL, 1)

    start, amount = by_group(start), by_group(amount)
    lanes = jnp.arange(CP, dtype=I32)
    slots = jnp.full((NG, M * BL, CP), -1, I32)
    for at in range(GT):
        rank = lanes - at * FOLD
        slots = jnp.where((rank >= 0) & (rank < jnp.minimum(amount[:, at], FOLD)), start[:, at] + rank, slots)
    reach = jnp.bitwise_xor(pairs.T[:, :, None], own_c)
    valid = (reach[:, :, None, :] == own_b[:, None]).astype(F32).reshape(T, M * BL, CP)

    all_kinds = jnp.sum(jnp.where(crossed[:, :, None] == labels, counts[:, None, None, :], 0), axis=3)
    before = jnp.sum(passed[None, :, :, :, None] * all_kinds[:, None, None], axis=3)
    least = jnp.min(before, axis=(0, 1, 3))
    most = jnp.max(before, axis=(0, 1, 3)) + jnp.max(counts)
    inside = (least >= jnp.array(SLOT_FROM)) & (most <= jnp.array(SLOT_TO))
    fits = jnp.all(inside) & (jnp.max(counts) <= FOLD)

    place = (jnp.minimum(ranks, FOLD) + jnp.where(ranks < FOLD, jnp.arange(G, dtype=I32)[:, None] * FOLD, V)).reshape(1, V)
    need = jnp.bitwise_xor(vir_irrep, occ_irrep[0]).reshape(1, V)
    have = jnp.bitwise_xor(own_c[:, None], occ_irrep[None, :]).reshape(1, CP * O)
    high, low = fold(place, need, have, cycle_weight.T)

    row_energy = (occ_energy[0] - lax.dynamic_slice_in_dim(vir_energy, g * CL, CL)).reshape(1, CL)
    slab_energy = lax.dynamic_slice_in_dim(vir_energy, m * BL, BL)
    col_energy = (occ_energy[None, :] - slab_energy[:, None]).reshape(J4, 1)
    row_need = jnp.bitwise_xor(own, occ_irrep[0]).reshape(1, CL)
    col_have = jnp.bitwise_xor(occ_irrep[None, :], own_b[:, None]).reshape(J4, 1)
    row_rank = own_rank.reshape(1, CL)
    slots, valid, fits, row_rank, row_need, col_have, row_energy, col_energy = lax.optimization_barrier(
        (slots, valid, fits, row_rank, row_need, col_have, row_energy, col_energy)
    )

    partial = contract(received, slots, valid, rank_c.reshape(1, CP), high, low)
    near = lax.ppermute(partial[1:3], "grp", [(d, d ^ 1) for d in range(G)])
    mine = partial[0] + near[0]
    last = lax.ppermute(partial[3] + near[1], "grp", [(d, d ^ 3) for d in range(G)])
    out = finish(mine, last, row_rank, row_need, col_have, row_energy, col_energy)
    return out.T, fits


def plain_form(amplitudes, cycle_weight, occ_irrep, vir_irrep, occ_energy, vir_energy):
    g = lax.axis_index("grp")
    m = lax.axis_index("blk")
    own = lax.dynamic_slice_in_dim(vir_irrep, g * CL, CL)
    own_b = lax.dynamic_slice_in_dim(vir_irrep, m * BL, BL)
    sent = jnp.transpose(amplitudes.reshape(T * CL, BW)).reshape(M, BL, T * CL)
    received = lax.all_to_all(sent, "blk", 0, 0, tiled=True)
    amp = jnp.transpose(received.reshape(M, BL, T, CL), (0, 2, 1, 3)).reshape(O, O, BL, CL)
    pairs = jnp.bitwise_xor(occ_irrep[:, None], occ_irrep[None, :])
    allowed = jnp.bitwise_xor(pairs[:, :, None], own_b)[..., None] == own
    amp = jnp.where(allowed, amp, jnp.zeros_like(amp))
    weight = cycle_weight.reshape(V, CL, O)
    need = jnp.bitwise_xor(vir_irrep, occ_irrep[0])
    have = jnp.bitwise_xor(own[:, None], occ_irrep[None, :])
    weight = jnp.where(need[:, None, None] == have, weight, jnp.zeros_like(weight))
    partial = jnp.einsum("kjbc,xck->xbj", amp, weight, precision=HIGHEST).reshape(G, CL, J4)
    cycle = jnp.sum(lax.all_to_all(partial, "grp", 0, 0, tiled=True).reshape(G, CL, J4), axis=0)
    row_energy = occ_energy[0] - lax.dynamic_slice_in_dim(vir_energy, g * CL, CL)
    slab_energy = lax.dynamic_slice_in_dim(vir_energy, m * BL, BL)
    col_energy = (occ_energy[None, :] - slab_energy[:, None]).reshape(J4)
    return cycle / (row_energy[:, None] + col_energy[None, :])


def shards(*arrays):
    out, fits = packed_form(*arrays)
    return lax.cond(fits, lambda: out, lambda: plain_form(*arrays))


def solution(mesh):
    in_specs = (P("blk", "grp", None), P(None, "grp"), P(), P(), P(), P())
    out_specs = P("grp", "blk")
    return jax.shard_map(shards, mesh=mesh, in_specs=in_specs, out_specs=out_specs, check_vma=False)
```

```python
import jax
import jax.numpy as jnp
from jax import lax
from jax.experimental import pallas as pl
from jax.experimental.pallas import tpu as pltpu
from jax.sharding import PartitionSpec as P

O = 40
V = 500
IW = 1
BW = 256
G = 4
M = 64
CL = V // G
CP = 128
T = O * O // M
TS = 5
BL = BW // M
J4 = O * BL
SLOTS = 640
FOLD = 40
NF = G * FOLD
GT = 3
NG = -(-T // GT)
STEP_SLOTS = ((0, 176), (16, 304), (48, 416), (112, 528), (160, SLOTS))
GROUP_BLOCKS = ((0, 1), (0, 2), (0, 3), (0, 3), (0, 4), (0, 4), (1, 5), (1, 5), (1, 5))
SLOT_FROM = tuple(max(CP * GROUP_BLOCKS[t // GT][0], STEP_SLOTS[t // TS][0]) for t in range(T))
SLOT_TO = tuple(min(CP * GROUP_BLOCKS[t // GT][1], STEP_SLOTS[t // TS][1]) for t in range(T))
NONE = 16

HIGHEST = lax.Precision.HIGHEST
F32 = jnp.float32
BF16 = jnp.bfloat16
I32 = jnp.int32


def dot(a, b):
    return jnp.dot(a, b, preferred_element_type=F32)


def halves(x):
    high = x.astype(BF16)
    return high, (x - high.astype(F32)).astype(BF16)


def in_hbm(x):
    return pltpu.with_memory_space_constraint(x, pltpu.HBM)


def iota(shape, dim):
    return lax.broadcasted_iota(I32, shape, dim)


def pack_kernel(occ_ref, vir_ref, amp_ref, out_ref, rank_ref, column_ref, count_ref, base_ref, total_ref, pick_ref, high_ref, low_ref):
    step = pl.program_id(0)
    g = lax.axis_index("grp")
    m = lax.axis_index("blk")
    row = vir_ref[:, 0:CP]
    for other in range(1, G):
        row = jnp.where(g == other, vir_ref[:, other * CL : other * CL + CP], row)
    row = jnp.where(iota((1, CP), 1) < CL, row, NONE)

    @pl.when(step == 0)
    def _():
        wide = jnp.broadcast_to(row, (CP, CP))
        column = jnp.transpose(wide)
        column_ref[...] = column
        before = (wide == column) & (iota((CP, CP), 0) < iota((CP, CP), 1))
        rank_ref[...] = jnp.sum(before.astype(F32), axis=0, keepdims=True).astype(I32)
        for q in range(8):
            same = (iota((8, CP), 0) == jnp.bitwise_xor(row, q)).astype(F32)
            count_ref[q] = jnp.broadcast_to(jnp.sum(same, axis=1, keepdims=True), (8, CP)).astype(I32)
        base_ref[...] = jnp.zeros_like(base_ref)
        total_ref[...] = jnp.zeros_like(total_ref)

    for phase, (first, last) in enumerate(STEP_SLOTS):

        @pl.when(step == phase)
        def _():
            for t in range(TS):
                pair = m * T + phase * TS + t
                q = jnp.bitwise_xor(occ_ref[pair // O], occ_ref[pair % O])
                same = iota((8, CP), 0) == jnp.bitwise_xor(row, q)
                base = jnp.sum(jnp.where(same, base_ref[...], 0).astype(F32), axis=0, keepdims=True).astype(I32)
                slot = base + rank_ref[...] - first
                base_ref[...] += count_ref[q]
                columns = slice(t * CP, (t + 1) * CP)
                pick_ref[0 : last - first, columns] = (iota((last - first, CP), 0) == slot).astype(F32).astype(BF16)
                need = jnp.bitwise_xor(column_ref[...], q)
                for half in range(BW // CP):
                    lanes = slice(half * CP, (half + 1) * CP)
                    block = jnp.where(need == vir_ref[:, lanes], amp_ref[t, :, lanes], 0.0)
                    high, low = halves(block)
                    high_ref[columns, lanes] = high
                    low_ref[columns, lanes] = low
            pick = pick_ref[0 : last - first]
            total_ref[first:last] += dot(pick, high_ref[...]) + dot(pick, low_ref[...])

    @pl.when(step == pl.num_programs(0) - 1)
    def _():
        out_ref[...] = jnp.transpose(total_ref[...]).reshape(M, BL, SLOTS)


def pack(occ_irrep, vir_row, amplitudes):
    return pl.pallas_call(
        pack_kernel,
        name="pack_amplitudes",
        grid=(T // TS,),
        out_shape=jax.ShapeDtypeStruct((M, BL, SLOTS), F32),
        in_specs=[
            pl.BlockSpec(memory_space=pltpu.SMEM),
            pl.BlockSpec((1, G * CP), lambda s: (0, 0)),
            pl.BlockSpec((TS, CP, BW), lambda s: (s, 0, 0)),
        ],
        out_specs=pl.BlockSpec((M, BL, SLOTS), lambda s: (0, 0, 0)),
        scratch_shapes=[
            pltpu.VMEM((1, CP), I32),
            pltpu.VMEM((CP, CP), I32),
            pltpu.VMEM((8, 8, CP), I32),
            pltpu.VMEM((8, CP), I32),
            pltpu.VMEM((SLOTS, BW), F32),
            pltpu.VMEM((SLOTS, TS * CP), BF16),
            pltpu.VMEM((TS * CP, BW), BF16),
            pltpu.VMEM((TS * CP, BW), BF16),
        ],
        compiler_params=pltpu.CompilerParams(vmem_limit_bytes=8 << 20),
    )(occ_irrep, vir_row, amplitudes)


CS = 16


def fold_kernel(place_ref, need_ref, have_ref, w_ref, high_ref, low_ref, pick_ref, turn_ref, rest_ref, first_ref, second_ref):
    step = pl.program_id(0)

    @pl.when(step == 0)
    def _():
        for first in range(0, V, CP):
            lanes = slice(first, min(first + CP, V))
            place = jnp.transpose(jnp.broadcast_to(place_ref[:, lanes], (CP, min(CP, V - first))))
            for at in range(0, NF, CP):
                wide = min(CP, NF - at)
                hit = iota((min(CP, V - first), wide), 1) + at == place[:, 0:wide]
                pick_ref[lanes, at : at + wide] = hit.astype(F32).astype(BF16)

    for part in range(CS * O // CP):
        rows = slice(part * CP, (part + 1) * CP)
        have = jnp.transpose(jnp.broadcast_to(have_ref[:, rows], (CP, CP)))
        for first in range(0, V, CP):
            lanes = slice(first, min(first + CP, V))
            kept = jnp.where(need_ref[:, lanes] == have[:, : min(CP, V - first)], w_ref[rows, lanes], 0.0)
            high, low = halves(kept)
            first_ref[rows, lanes] = high
            second_ref[rows, lanes] = low
    folded = dot(first_ref[...], pick_ref[...]) + dot(second_ref[...], pick_ref[...])
    turn_ref[...] = folded[:, 0:CP]
    rest_ref[:, 0 : NF - CP] = folded[:, CP:NF]
    for k in range(O):
        rows = pl.ds(k, CS, stride=O)
        part = jnp.concatenate([turn_ref[rows, :], rest_ref[rows, :]], axis=1)
        high, low = halves(part[:, 0:NF])
        high_ref[k] = high
        low_ref[k] = low


def fold(place, need, have, turned_weight):
    rows = CS * O
    out = pltpu.HBM((O, CP, NF), BF16)
    spec = pl.BlockSpec((O, CS, NF), lambda s: (0, s, 0))
    return pl.pallas_call(
        fold_kernel,
        name="fold_weights",
        grid=(CP // CS,),
        out_shape=(out, out),
        in_specs=[
            pl.BlockSpec((1, V), lambda s: (0, 0)),
            pl.BlockSpec((1, V), lambda s: (0, 0)),
            pl.BlockSpec((1, rows), lambda s: (0, s)),
            pl.BlockSpec((rows, V), lambda s: (s, 0)),
        ],
        out_specs=(spec, spec),
        scratch_shapes=[pltpu.VMEM((V, NF), BF16), pltpu.VMEM((rows, CP), F32), pltpu.VMEM((rows, CP), F32)]
        + [pltpu.VMEM((rows, V), BF16)] * 2,
        compiler_params=pltpu.CompilerParams(vmem_limit_bytes=8 << 20),
    )(place, need, have, turned_weight)


def amounts(kinds, counts_ref, g):
    found = jnp.zeros(kinds.shape, I32)
    for label in range(8):
        found = jnp.where(kinds == label, counts_ref[g, label], found)
    return found.astype(F32).astype(BF16)


def table_kernel(counts_ref, mine_ref, all_ref, c_ref, from_ref, to_ref, slot_ref, valid_ref, fits_ref):
    g = lax.axis_index("grp")
    mine = mine_ref[...]
    held = amounts(mine, counts_ref, g)
    pair = iota((T, CP), 0)
    at = iota((T, CP), 1) // FOLD
    rank = iota((M * BL, CP), 1) % FOLD
    real = iota((M * BL, CP), 1) < GT * FOLD
    for group in range(NG):
        start = dot(held, (pair < GT * group + at).astype(F32).astype(BF16)).astype(I32)
        amount = dot(held, (pair == GT * group + at).astype(F32).astype(BF16)).astype(I32)
        slot_ref[group] = jnp.where(real & (rank < amount), start + rank, -1)
    label = mine.astype(F32).astype(BF16)
    for t in range(T):
        wide = dot(label, (pair == t).astype(F32).astype(BF16)).astype(I32)
        valid_ref[t] = (wide == c_ref[...]).astype(F32)
    good = jnp.ones((8 * M, T), F32)
    earlier = (iota((T, T), 0) < iota((T, T), 1)).astype(F32).astype(BF16)
    most = counts_ref[0, 0]
    for other in range(G):
        for label in range(8):
            most = jnp.maximum(most, counts_ref[other, label])
    for other in range(G):
        start = dot(amounts(all_ref[...], counts_ref, other), earlier).astype(I32)
        good = jnp.where((start >= from_ref[...]) & (start + most <= to_ref[...]), good, 0.0)
    fits = jnp.min(good, axis=(0, 1), keepdims=True)
    fits = jnp.where(most <= FOLD, fits, 0.0)
    fits_ref[...] = jnp.broadcast_to(fits, (8, CP))


def tables(counts, mine, every, own_c, low, high):
    vmem = pl.BlockSpec(memory_space=pltpu.VMEM)
    return pl.pallas_call(
        table_kernel,
        name="tables",
        out_shape=(
            pltpu.HBM((NG, M * BL, CP), I32),
            jax.ShapeDtypeStruct((T, M * BL, CP), F32),
            jax.ShapeDtypeStruct((8, CP), F32),
        ),
        in_specs=[pl.BlockSpec(memory_space=pltpu.SMEM)] + [vmem] * 5,
        compiler_params=pltpu.CompilerParams(vmem_limit_bytes=8 << 20),
    )(counts, mine, every, own_c, low, high)


def contract_kernel(
    far_x_ref, far_slot_ref, valid_ref, rank_ref, far_high_ref, far_low_ref, out_ref,
    x_ref, slot_ref, seen_ref, spread_ref, wide_ref, high_ref, low_ref, sem,
):
    g = lax.axis_index("grp")
    first_copies = [
        pltpu.make_async_copy(far_x_ref, x_ref, sem.at[2]),
        pltpu.make_async_copy(far_slot_ref, slot_ref, sem.at[3]),
    ]
    copies = [
        pltpu.make_async_copy(far_high_ref, high_ref, sem.at[0]),
        pltpu.make_async_copy(far_low_ref, low_ref, sem.at[1]),
    ]
    for copy in first_copies + copies:
        copy.start()
    for copy in first_copies:
        copy.wait()

    @pl.loop(0, M // 8)
    def _(i):
        for near in range(4):
            packed = x_ref[pl.ds(8 * i + 2 * near, 2)].reshape(2 * BL, SLOTS)
            rows = pl.ds(pl.multiple_of(32 * i, 8) + 8 * near, 8)
            for group, (first, last) in enumerate(GROUP_BLOCKS):
                slot = slot_ref[group, rows, :]
                lane = jnp.bitwise_and(slot, CP - 1)
                where = jnp.right_shift(slot, 7)
                found = jnp.zeros((8, CP), F32)
                for part in range(first, last):
                    taken = jnp.take_along_axis(
                        packed[:, part * CP : (part + 1) * CP], lane, axis=1, mode="promise_in_bounds"
                    )
                    found = jnp.where(where == part, taken, found)
                seen_ref[group, rows, :] = found

    place = [(iota((CP, CP), 0) - at * FOLD == rank_ref[...]).astype(F32).astype(BF16) for at in range(GT)]
    place = jnp.concatenate(place, axis=1)
    place = jnp.concatenate([place, place], axis=0)
    for group in range(NG):
        spread_ref[group] = dot(jnp.concatenate(halves(seen_ref[group]), axis=1), place)

    @pl.loop(0, M // 2)
    def _(i):
        rows = pl.ds(pl.multiple_of(8 * i, 8), 8)
        first = pl.multiple_of(2 * T * BL * i, 8)
        for t in range(T):
            at = (t % GT) * CP
            row = spread_ref[t // GT, rows, at : at + CP] * valid_ref[t, rows, :]
            if t % 2 == 0:
                one, two = row[0:BL], row[BL : 2 * BL]
            else:
                row = pltpu.roll(row, BL, 0)
                one, two = row[BL : 2 * BL], row[0:BL]
            wide_ref[pl.ds(first + BL * t, BL), :] = one
            wide_ref[pl.ds(first + T * BL + BL * t, BL), :] = two

    for copy in copies:
        copy.wait()
    total = jnp.zeros((J4, NF), F32)
    for i in range(O // 2):
        first = 2 * J4 * i
        amp = jnp.concatenate([wide_ref[first : first + J4], wide_ref[first + J4 : first + 2 * J4]], axis=1)
        a_high, a_low = halves(amp)
        w_high = high_ref[2 * i : 2 * i + 2].reshape(2 * CP, NF)
        w_low = low_ref[2 * i : 2 * i + 2].reshape(2 * CP, NF)
        both = dot(jnp.concatenate([a_high, a_low], axis=0), w_high)
        total = total + (both[0:J4] + both[J4 : 2 * J4] + dot(a_high, w_low))

    turned = jnp.transpose(total)
    for block in range(G):
        out_ref[jnp.bitwise_xor(g, block)] = turned[block * FOLD : (block + 1) * FOLD]


def contract(received, slots, valid, rank, high, low):
    vmem = pl.BlockSpec(memory_space=pltpu.VMEM)
    hbm = pl.BlockSpec(memory_space=pltpu.HBM)
    return pl.pallas_call(
        contract_kernel,
        name="contract",
        out_shape=jax.ShapeDtypeStruct((G, FOLD, J4), F32),
        in_specs=[hbm, hbm, vmem, vmem, hbm, hbm],
        scratch_shapes=[
            pltpu.VMEM((M, BL, SLOTS), F32),
            pltpu.VMEM((NG, M * BL, CP), I32),
            pltpu.VMEM((NG, M * BL, CP), F32),
            pltpu.VMEM((NG, M * BL, GT * CP), F32),
            pltpu.VMEM((O * O * BL, CP), F32),
            pltpu.VMEM((O, CP, NF), BF16),
            pltpu.VMEM((O, CP, NF), BF16),
            pltpu.SemaphoreType.DMA((4,)),
        ],
        compiler_params=pltpu.CompilerParams(vmem_limit_bytes=20 << 20),
    )(in_hbm(received), in_hbm(slots), valid, rank, in_hbm(high), in_hbm(low))


def finish_kernel(a_ref, b_ref, rank_ref, need_ref, have_ref, row_ref, column_ref, out_ref):
    folded = a_ref[...] + b_ref[...]
    source = iota((J4, J4), 0)
    target = iota((J4, J4), 1)
    move = (source % BL) * O + source // BL == target
    folded = jnp.dot(folded, move.astype(F32), precision=HIGHEST, preferred_element_type=F32)
    pick = (iota((FOLD, CL), 0) == rank_ref[...]).astype(F32)
    wide = jnp.dot(jnp.transpose(folded), pick, precision=HIGHEST, preferred_element_type=F32)
    wide = jnp.where(need_ref[...] == have_ref[...], wide, 0.0)
    out_ref[...] = wide / (row_ref[...] + column_ref[...])


def finish(a, b, rank, need, have, row, column):
    return pl.pallas_call(
        finish_kernel,
        name="finish",
        out_shape=pltpu.HBM((J4, CL), F32),
        compiler_params=pltpu.CompilerParams(vmem_limit_bytes=4 << 20),
    )(a, b, rank, need, have, row, column)


def packed_form(amplitudes, cycle_weight, occ_irrep, vir_irrep, occ_energy, vir_energy):
    g = lax.axis_index("grp")
    m = lax.axis_index("blk")
    labels = jnp.arange(8, dtype=I32)
    sent = pack(occ_irrep, vir_irrep.reshape(1, V), amplitudes)
    received = lax.all_to_all(sent, "blk", 0, 0, tiled=True)

    shares = vir_irrep.reshape(G, CL)
    orbital = jnp.arange(CL)
    earlier = orbital[:, None] < orbital[None, :]
    ranks = jnp.sum((shares[:, :, None] == shares[:, None, :]) & earlier[None], axis=1).astype(I32)
    counts = jnp.sum(shares[:, :, None] == labels, axis=1).astype(I32)
    own = lax.dynamic_index_in_dim(shares, g, 0, keepdims=False)
    own_rank = lax.dynamic_index_in_dim(ranks, g, 0, keepdims=False)
    own_c = jnp.concatenate([own, jnp.full((CP - CL,), NONE, I32)])
    rank_c = jnp.concatenate([own_rank, jnp.zeros((CP - CL,), I32)])

    pairs = jnp.bitwise_xor(occ_irrep[:, None], occ_irrep[None, :]).reshape(M, 1, T)
    own_b = lax.dynamic_slice_in_dim(vir_irrep, m * BL, BL)
    mine = jnp.bitwise_xor(pairs, own_b[:, None]).reshape(M * BL, T)
    every = jnp.bitwise_xor(pairs, labels[:, None]).reshape(M * 8, T)
    low, high = (jnp.array(x, I32).reshape(1, T) for x in (SLOT_FROM, SLOT_TO))
    slots, valid, fits = tables(counts, mine, every, own_c.reshape(1, CP), low, high)
    fits = fits[0, 0] > 0.5

    place = (jnp.minimum(ranks, FOLD) + jnp.where(ranks < FOLD, jnp.arange(G, dtype=I32)[:, None] * FOLD, V)).reshape(1, V)
    need = jnp.bitwise_xor(vir_irrep, occ_irrep[0]).reshape(1, V)
    have = jnp.bitwise_xor(own_c[:, None], occ_irrep[None, :]).reshape(1, CP * O)
    high, low = fold(place, need, have, cycle_weight.T)

    row_energy = (occ_energy[0] - lax.dynamic_slice_in_dim(vir_energy, g * CL, CL)).reshape(1, CL)
    slab_energy = lax.dynamic_slice_in_dim(vir_energy, m * BL, BL)
    col_energy = (occ_energy[None, :] - slab_energy[:, None]).reshape(J4, 1)
    row_need = jnp.bitwise_xor(own, occ_irrep[0]).reshape(1, CL)
    col_have = jnp.bitwise_xor(occ_irrep[None, :], own_b[:, None]).reshape(J4, 1)
    row_rank = own_rank.reshape(1, CL)
    slots, valid, fits, row_rank, row_need, col_have, row_energy, col_energy = lax.optimization_barrier(
        (slots, valid, fits, row_rank, row_need, col_have, row_energy, col_energy)
    )

    partial = contract(received, slots, valid, rank_c.reshape(1, CP), high, low)
    near = lax.ppermute(partial[1:3], "grp", [(d, d ^ 1) for d in range(G)])
    mine = partial[0] + near[0]
    last = lax.ppermute(partial[3] + near[1], "grp", [(d, d ^ 3) for d in range(G)])
    out = finish(mine, last, row_rank, row_need, col_have, row_energy, col_energy)
    return out.T, fits


def plain_form(amplitudes, cycle_weight, occ_irrep, vir_irrep, occ_energy, vir_energy):
    g = lax.axis_index("grp")
    m = lax.axis_index("blk")
    own = lax.dynamic_slice_in_dim(vir_irrep, g * CL, CL)
    own_b = lax.dynamic_slice_in_dim(vir_irrep, m * BL, BL)
    sent = jnp.transpose(amplitudes.reshape(T * CL, BW)).reshape(M, BL, T * CL)
    received = lax.all_to_all(sent, "blk", 0, 0, tiled=True)
    amp = jnp.transpose(received.reshape(M, BL, T, CL), (0, 2, 1, 3)).reshape(O, O, BL, CL)
    pairs = jnp.bitwise_xor(occ_irrep[:, None], occ_irrep[None, :])
    allowed = jnp.bitwise_xor(pairs[:, :, None], own_b)[..., None] == own
    amp = jnp.where(allowed, amp, jnp.zeros_like(amp))
    weight = cycle_weight.reshape(V, CL, O)
    need = jnp.bitwise_xor(vir_irrep, occ_irrep[0])
    have = jnp.bitwise_xor(own[:, None], occ_irrep[None, :])
    weight = jnp.where(need[:, None, None] == have, weight, jnp.zeros_like(weight))
    partial = jnp.einsum("kjbc,xck->xbj", amp, weight, precision=HIGHEST).reshape(G, CL, J4)
    cycle = jnp.sum(lax.all_to_all(partial, "grp", 0, 0, tiled=True).reshape(G, CL, J4), axis=0)
    row_energy = occ_energy[0] - lax.dynamic_slice_in_dim(vir_energy, g * CL, CL)
    slab_energy = lax.dynamic_slice_in_dim(vir_energy, m * BL, BL)
    col_energy = (occ_energy[None, :] - slab_energy[:, None]).reshape(J4)
    return cycle / (row_energy[:, None] + col_energy[None, :])


def shards(*arrays):
    out, fits = packed_form(*arrays)
    return lax.cond(fits, lambda: out, lambda: plain_form(*arrays))


def solution(mesh):
    in_specs = (P("blk", "grp", None), P(None, "grp"), P(), P(), P(), P())
    out_specs = P("grp", "blk")
    return jax.shard_map(shards, mesh=mesh, in_specs=in_specs, out_specs=out_specs, check_vma=False)
```

```python
import jax
import jax.numpy as jnp
from jax import lax
from jax.experimental import pallas as pl
from jax.experimental.pallas import tpu as pltpu
from jax.sharding import PartitionSpec as P

O = 40
V = 500
IW = 1
BW = 256
G = 4
M = 64
CL = V // G
CP = 128
T = O * O // M
TS = 5
BL = BW // M
J4 = O * BL
SLOTS = 640
FOLD = 40
NF = G * FOLD
GT = 3
NG = -(-T // GT)
STEP_SLOTS = ((0, 176), (16, 304), (48, 416), (112, 528), (160, SLOTS))
GROUP_BLOCKS = ((0, 1), (0, 2), (0, 3), (0, 3), (0, 4), (0, 4), (1, 5), (1, 5), (1, 5))
SLOT_FROM = tuple(max(CP * GROUP_BLOCKS[t // GT][0], STEP_SLOTS[t // TS][0]) for t in range(T))
SLOT_TO = tuple(min(CP * GROUP_BLOCKS[t // GT][1], STEP_SLOTS[t // TS][1]) for t in range(T))
NONE = 16

HIGHEST = lax.Precision.HIGHEST
F32 = jnp.float32
BF16 = jnp.bfloat16
I32 = jnp.int32


def dot(a, b):
    return jnp.dot(a, b, preferred_element_type=F32)


def halves(x):
    high = x.astype(BF16)
    return high, (x - high.astype(F32)).astype(BF16)


def in_hbm(x):
    return pltpu.with_memory_space_constraint(x, pltpu.HBM)


def share_of(ref, share):
    first = share * CL
    over = first - (V - CP)
    if over <= 0:
        return ref[:, first : first + CP]
    return pltpu.roll(ref[:, V - CP : V], CP - over, 1)


def own_share(ref, g):
    row = share_of(ref, 0)
    for share in range(1, G):
        row = jnp.where(g == share, share_of(ref, share), row)
    return row


def labels_of(row):
    return jnp.where(iota((1, CP), 1) < CL, row, NONE)


def same_before(row):
    wide = jnp.broadcast_to(row, (CP, CP))
    return ((wide == jnp.transpose(wide)) & (iota((CP, CP), 0) < iota((CP, CP), 1))).astype(F32)


def one_hot(x):
    return x.astype(F32).astype(BF16)


def iota(shape, dim):
    return lax.broadcasted_iota(I32, shape, dim)


def pack_kernel(occ_ref, vir_ref, amp_ref, out_ref, rank_ref, column_ref, count_ref, base_ref, total_ref, pick_ref, high_ref, low_ref):
    step = pl.program_id(0)
    g = lax.axis_index("grp")
    m = lax.axis_index("blk")
    row = vir_ref[:, 0:CP]
    for other in range(1, G):
        row = jnp.where(g == other, vir_ref[:, other * CL : other * CL + CP], row)
    row = jnp.where(iota((1, CP), 1) < CL, row, NONE)

    @pl.when(step == 0)
    def _():
        wide = jnp.broadcast_to(row, (CP, CP))
        column = jnp.transpose(wide)
        column_ref[...] = column
        before = (wide == column) & (iota((CP, CP), 0) < iota((CP, CP), 1))
        rank_ref[...] = jnp.sum(before.astype(F32), axis=0, keepdims=True).astype(I32)
        for q in range(8):
            same = (iota((8, CP), 0) == jnp.bitwise_xor(row, q)).astype(F32)
            count_ref[q] = jnp.broadcast_to(jnp.sum(same, axis=1, keepdims=True), (8, CP)).astype(I32)
        base_ref[...] = jnp.zeros_like(base_ref)
        total_ref[...] = jnp.zeros_like(total_ref)

    for phase, (first, last) in enumerate(STEP_SLOTS):

        @pl.when(step == phase)
        def _():
            for t in range(TS):
                pair = m * T + phase * TS + t
                q = jnp.bitwise_xor(occ_ref[pair // O], occ_ref[pair % O])
                same = iota((8, CP), 0) == jnp.bitwise_xor(row, q)
                base = jnp.sum(jnp.where(same, base_ref[...], 0).astype(F32), axis=0, keepdims=True).astype(I32)
                slot = base + rank_ref[...] - first
                base_ref[...] += count_ref[q]
                columns = slice(t * CP, (t + 1) * CP)
                pick_ref[0 : last - first, columns] = (iota((last - first, CP), 0) == slot).astype(F32).astype(BF16)
                need = jnp.bitwise_xor(column_ref[...], q)
                for half in range(BW // CP):
                    lanes = slice(half * CP, (half + 1) * CP)
                    block = jnp.where(need == vir_ref[:, lanes], amp_ref[t, :, lanes], 0.0)
                    high, low = halves(block)
                    high_ref[columns, lanes] = high
                    low_ref[columns, lanes] = low
            pick = pick_ref[0 : last - first]
            total_ref[first:last] += dot(pick, high_ref[...]) + dot(pick, low_ref[...])

    @pl.when(step == pl.num_programs(0) - 1)
    def _():
        out_ref[...] = jnp.transpose(total_ref[...]).reshape(M, BL, SLOTS)


def pack(occ_irrep, vir_row, amplitudes):
    return pl.pallas_call(
        pack_kernel,
        name="pack_amplitudes",
        grid=(T // TS,),
        out_shape=jax.ShapeDtypeStruct((M, BL, SLOTS), F32),
        in_specs=[
            pl.BlockSpec(memory_space=pltpu.SMEM),
            pl.BlockSpec((1, G * CP), lambda s: (0, 0)),
            pl.BlockSpec((TS, CP, BW), lambda s: (s, 0, 0)),
        ],
        out_specs=pl.BlockSpec((M, BL, SLOTS), lambda s: (0, 0, 0)),
        scratch_shapes=[
            pltpu.VMEM((1, CP), I32),
            pltpu.VMEM((CP, CP), I32),
            pltpu.VMEM((8, 8, CP), I32),
            pltpu.VMEM((8, CP), I32),
            pltpu.VMEM((SLOTS, BW), F32),
            pltpu.VMEM((SLOTS, TS * CP), BF16),
            pltpu.VMEM((TS * CP, BW), BF16),
            pltpu.VMEM((TS * CP, BW), BF16),
        ],
        compiler_params=pltpu.CompilerParams(vmem_limit_bytes=8 << 20),
    )(occ_irrep, vir_row, amplitudes)


CS = 16


def fold_kernel(
    occ_ref, vir_ref, have_ref, w_ref, high_ref, low_ref, lay_ref, pick_ref, turn_ref, rest_ref, first_ref, second_ref
):
    step = pl.program_id(0)

    @pl.when(step == 0)
    def _():
        for share in range(G):
            before = jnp.transpose(same_before(labels_of(share_of(vir_ref, share))))
            rank = jnp.sum(before, axis=1, keepdims=True).astype(I32)
            hit = (iota((CP, NF), 1) == rank + share * FOLD) & (rank < FOLD)
            lay_ref[share * CL : share * CL + CP, :] = hit.astype(F32)
        pick_ref[...] = lay_ref[...].astype(BF16)

    need = jnp.bitwise_xor(vir_ref[...], occ_ref[0])
    for part in range(CS * O // CP):
        rows = slice(part * CP, (part + 1) * CP)
        have = jnp.transpose(jnp.broadcast_to(have_ref[:, rows], (CP, CP)))
        for first in range(0, V, CP):
            lanes = slice(first, min(first + CP, V))
            kept = jnp.where(need[:, lanes] == have[:, : min(CP, V - first)], w_ref[rows, lanes], 0.0)
            high, low = halves(kept)
            first_ref[rows, lanes] = high
            second_ref[rows, lanes] = low
    folded = dot(first_ref[...], pick_ref[0:V]) + dot(second_ref[...], pick_ref[0:V])
    turn_ref[...] = folded[:, 0:CP]
    rest_ref[:, 0 : NF - CP] = folded[:, CP:NF]
    for k in range(O):
        rows = pl.ds(k, CS, stride=O)
        part = jnp.concatenate([turn_ref[rows, :], rest_ref[rows, :]], axis=1)
        high, low = halves(part[:, 0:NF])
        high_ref[k] = high
        low_ref[k] = low


def fold(occ_irrep, vir_row, have, turned_weight):
    rows = CS * O
    out = pltpu.HBM((O, CP, NF), BF16)
    spec = pl.BlockSpec((O, CS, NF), lambda s: (0, s, 0))
    return pl.pallas_call(
        fold_kernel,
        name="fold_weights",
        grid=(CP // CS,),
        out_shape=(out, out),
        in_specs=[
            pl.BlockSpec(memory_space=pltpu.SMEM),
            pl.BlockSpec((1, V), lambda s: (0, 0)),
            pl.BlockSpec((1, rows), lambda s: (0, s)),
            pl.BlockSpec((rows, V), lambda s: (s, 0)),
        ],
        out_specs=(spec, spec),
        scratch_shapes=[pltpu.VMEM((G * CP, NF), F32), pltpu.VMEM((G * CP, NF), BF16), pltpu.VMEM((rows, CP), F32), pltpu.VMEM((rows, CP), F32)]
        + [pltpu.VMEM((rows, V), BF16)] * 2,
        compiler_params=pltpu.CompilerParams(vmem_limit_bytes=8 << 20),
    )(occ_irrep, vir_row, have, turned_weight)


def amounts(kinds, counts):
    found = jnp.zeros(kinds.shape, I32)
    for label in range(8):
        found = jnp.where(kinds == label, counts[label], found)
    return one_hot(found)


def table_kernel(
    occ_ref, vir_ref, occ_energy_ref, vir_energy_ref, vir_row_ref, energy_row_ref, from_ref, to_ref,
    slot_ref, valid_ref, fits_ref, rank_ref, pick_ref, keep_ref, divisor_ref,
):
    g = lax.axis_index("grp")
    m = lax.axis_index("blk")
    own = labels_of(own_share(vir_row_ref, g))
    rank = jnp.sum(same_before(own), axis=0, keepdims=True).astype(I32)
    rank_ref[...] = rank
    pick_ref[...] = (iota((FOLD, CP), 0) == rank).astype(F32)

    counts = []
    for share in range(G):
        row = labels_of(share_of(vir_row_ref, share))
        counts.append([jnp.sum((row == label).astype(F32), axis=1, keepdims=True).astype(I32) for label in range(8)])
    held = counts[0]
    for share in range(1, G):
        held = [jnp.where(g == share, new, old) for new, old in zip(counts[share], held)]

    number = iota((M, T), 0) * T + iota((M, T), 1)
    k, j = number // O, number % O
    kind_k, kind_j = jnp.zeros((M, T), I32), jnp.zeros((M, T), I32)
    for o in range(O):
        kind_k = jnp.where(k == o, occ_ref[o], kind_k)
        kind_j = jnp.where(j == o, occ_ref[o], kind_j)
    kinds = one_hot(jnp.bitwise_xor(kind_k, kind_j))
    rows = iota((M * BL, 1), 0)
    label = jnp.zeros((M * BL, 1), I32)
    for b in range(BL):
        label = jnp.where(rows % BL == b, vir_ref[m * BL + b], label)
    mine = dot(one_hot(iota((M * BL, M), 0) // BL == iota((M * BL, M), 1)), kinds).astype(I32)
    mine = jnp.bitwise_xor(mine, label)
    every = dot(one_hot(iota((M * 8, M), 0) // 8 == iota((M * 8, M), 1)), kinds).astype(I32)
    every = jnp.bitwise_xor(every, iota((M * 8, 1), 0) % 8)

    amount_of = amounts(mine, held)
    pair = iota((T, CP), 0)
    at = iota((T, CP), 1) // FOLD
    place = iota((M * BL, CP), 1) % FOLD
    real = iota((M * BL, CP), 1) < GT * FOLD
    for group in range(NG):
        start = dot(amount_of, one_hot(pair < GT * group + at)).astype(I32)
        amount = dot(amount_of, one_hot(pair == GT * group + at)).astype(I32)
        slot_ref[group] = jnp.where(real & (place < amount), start + place, -1)
    mine = one_hot(mine)
    for t in range(T):
        valid_ref[t] = (dot(mine, one_hot(pair == t)).astype(I32) == own).astype(F32)

    most = counts[0][0]
    for share in range(G):
        for count in counts[share]:
            most = jnp.maximum(most, count)
    good = jnp.ones((8 * M, T), F32)
    earlier = one_hot(iota((T, T), 0) < iota((T, T), 1))
    for share in range(G):
        start = dot(amounts(every, counts[share]), earlier).astype(I32)
        good = jnp.where((start >= from_ref[...]) & (start + most <= to_ref[...]), good, 0.0)
    fits = jnp.where(most <= FOLD, jnp.min(good, axis=(0, 1), keepdims=True), 0.0)
    fits_ref[...] = jnp.broadcast_to(fits, (8, CP))

    row = iota((J4, CP), 0)
    occ_label, occ_energy = jnp.zeros((J4, CP), I32), jnp.zeros((J4, CP), F32)
    for o in range(O):
        occ_label = jnp.where(row % O == o, occ_ref[o], occ_label)
        occ_energy = jnp.where(row % O == o, occ_energy_ref[o], occ_energy)
    vir_label, vir_energy = jnp.zeros((J4, CP), I32), jnp.zeros((J4, CP), F32)
    for b in range(BL):
        vir_label = jnp.where(row // O == b, vir_ref[m * BL + b], vir_label)
        vir_energy = jnp.where(row // O == b, vir_energy_ref[m * BL + b], vir_energy)
    need = jnp.bitwise_xor(own, occ_ref[0])
    keep_ref[...] = (need == jnp.bitwise_xor(occ_label, vir_label)).astype(F32)
    row_energy = occ_energy_ref[0] - own_share(energy_row_ref, g)
    divisor_ref[...] = row_energy + (occ_energy - vir_energy)


def tables(occ_irrep, vir_irrep, occ_energy, vir_energy):
    smem = pl.BlockSpec(memory_space=pltpu.SMEM)
    vmem = pl.BlockSpec(memory_space=pltpu.VMEM)
    low, high = (jnp.array(x, I32).reshape(1, T) for x in (SLOT_FROM, SLOT_TO))
    return pl.pallas_call(
        table_kernel,
        name="tables",
        out_shape=(
            pltpu.HBM((NG, M * BL, CP), I32),
            jax.ShapeDtypeStruct((T, M * BL, CP), F32),
            jax.ShapeDtypeStruct((8, CP), F32),
            jax.ShapeDtypeStruct((1, CP), I32),
            jax.ShapeDtypeStruct((FOLD, CP), F32),
            jax.ShapeDtypeStruct((J4, CP), F32),
            jax.ShapeDtypeStruct((J4, CP), F32),
        ),
        in_specs=[smem] * 4 + [vmem] * 4,
        compiler_params=pltpu.CompilerParams(vmem_limit_bytes=8 << 20),
    )(occ_irrep, vir_irrep, occ_energy, vir_energy, vir_irrep.reshape(1, V), vir_energy.reshape(1, V), low, high)


def contract_kernel(
    far_x_ref, far_slot_ref, valid_ref, rank_ref, far_high_ref, far_low_ref, out_ref,
    x_ref, slot_ref, seen_ref, spread_ref, wide_ref, high_ref, low_ref, sem,
):
    g = lax.axis_index("grp")
    first_copies = [
        pltpu.make_async_copy(far_x_ref, x_ref, sem.at[2]),
        pltpu.make_async_copy(far_slot_ref, slot_ref, sem.at[3]),
    ]
    copies = [
        pltpu.make_async_copy(far_high_ref, high_ref, sem.at[0]),
        pltpu.make_async_copy(far_low_ref, low_ref, sem.at[1]),
    ]
    for copy in first_copies + copies:
        copy.start()
    for copy in first_copies:
        copy.wait()

    @pl.loop(0, M // 8)
    def _(i):
        for near in range(4):
            packed = x_ref[pl.ds(8 * i + 2 * near, 2)].reshape(2 * BL, SLOTS)
            rows = pl.ds(pl.multiple_of(32 * i, 8) + 8 * near, 8)
            for group, (first, last) in enumerate(GROUP_BLOCKS):
                slot = slot_ref[group, rows, :]
                lane = jnp.bitwise_and(slot, CP - 1)
                where = jnp.right_shift(slot, 7)
                found = jnp.zeros((8, CP), F32)
                for part in range(first, last):
                    taken = jnp.take_along_axis(
                        packed[:, part * CP : (part + 1) * CP], lane, axis=1, mode="promise_in_bounds"
                    )
                    found = jnp.where(where == part, taken, found)
                seen_ref[group, rows, :] = found

    place = [(iota((CP, CP), 0) - at * FOLD == rank_ref[...]).astype(F32).astype(BF16) for at in range(GT)]
    place = jnp.concatenate(place, axis=1)
    place = jnp.concatenate([place, place], axis=0)
    for group in range(NG):
        spread_ref[group] = dot(jnp.concatenate(halves(seen_ref[group]), axis=1), place)

    @pl.loop(0, M // 2)
    def _(i):
        rows = pl.ds(pl.multiple_of(8 * i, 8), 8)
        first = pl.multiple_of(2 * T * BL * i, 8)
        for t in range(T):
            at = (t % GT) * CP
            row = spread_ref[t // GT, rows, at : at + CP] * valid_ref[t, rows, :]
            if t % 2 == 0:
                one, two = row[0:BL], row[BL : 2 * BL]
            else:
                row = pltpu.roll(row, BL, 0)
                one, two = row[BL : 2 * BL], row[0:BL]
            wide_ref[pl.ds(first + BL * t, BL), :] = one
            wide_ref[pl.ds(first + T * BL + BL * t, BL), :] = two

    for copy in copies:
        copy.wait()
    total = jnp.zeros((J4, NF), F32)
    for i in range(O // 2):
        first = 2 * J4 * i
        amp = jnp.concatenate([wide_ref[first : first + J4], wide_ref[first + J4 : first + 2 * J4]], axis=1)
        a_high, a_low = halves(amp)
        w_high = high_ref[2 * i : 2 * i + 2].reshape(2 * CP, NF)
        w_low = low_ref[2 * i : 2 * i + 2].reshape(2 * CP, NF)
        both = dot(jnp.concatenate([a_high, a_low], axis=0), w_high)
        total = total + (both[0:J4] + both[J4 : 2 * J4] + dot(a_high, w_low))

    turned = jnp.transpose(total)
    for block in range(G):
        out_ref[jnp.bitwise_xor(g, block)] = turned[block * FOLD : (block + 1) * FOLD]


def contract(received, slots, valid, rank, high, low):
    vmem = pl.BlockSpec(memory_space=pltpu.VMEM)
    hbm = pl.BlockSpec(memory_space=pltpu.HBM)
    return pl.pallas_call(
        contract_kernel,
        name="contract",
        out_shape=jax.ShapeDtypeStruct((G, FOLD, J4), F32),
        in_specs=[hbm, hbm, vmem, vmem, hbm, hbm],
        scratch_shapes=[
            pltpu.VMEM((M, BL, SLOTS), F32),
            pltpu.VMEM((NG, M * BL, CP), I32),
            pltpu.VMEM((NG, M * BL, CP), F32),
            pltpu.VMEM((NG, M * BL, GT * CP), F32),
            pltpu.VMEM((O * O * BL, CP), F32),
            pltpu.VMEM((O, CP, NF), BF16),
            pltpu.VMEM((O, CP, NF), BF16),
            pltpu.SemaphoreType.DMA((4,)),
        ],
        compiler_params=pltpu.CompilerParams(vmem_limit_bytes=20 << 20),
    )(in_hbm(received), in_hbm(slots), valid, rank, in_hbm(high), in_hbm(low))


def finish_kernel(a_ref, b_ref, pick_ref, keep_ref, divisor_ref, out_ref):
    folded = a_ref[...] + b_ref[...]
    source = iota((J4, J4), 0)
    target = iota((J4, J4), 1)
    move = (source % BL) * O + source // BL == target
    folded = jnp.dot(folded, move.astype(F32), precision=HIGHEST, preferred_element_type=F32)
    wide = jnp.dot(jnp.transpose(folded), pick_ref[...], precision=HIGHEST, preferred_element_type=F32)
    wide = jnp.where(keep_ref[...] > 0, wide, 0.0) / divisor_ref[...]
    out_ref[...] = wide[:, 0:CL]


def finish(a, b, pick, keep, divisor):
    return pl.pallas_call(
        finish_kernel,
        name="finish",
        out_shape=pltpu.HBM((J4, CL), F32),
        compiler_params=pltpu.CompilerParams(vmem_limit_bytes=4 << 20),
    )(a, b, pick, keep, divisor)


def packed_form(amplitudes, cycle_weight, occ_irrep, vir_irrep, occ_energy, vir_energy):
    g = lax.axis_index("grp")
    vir_row = vir_irrep.reshape(1, V)
    sent = pack(occ_irrep, vir_row, amplitudes)
    received = lax.all_to_all(sent, "blk", 0, 0, tiled=True)

    slots, valid, fits, rank, pick, keep, divisor = tables(occ_irrep, vir_irrep, occ_energy, vir_energy)
    own = lax.dynamic_slice_in_dim(jnp.pad(vir_irrep, (0, CP - CL)), g * CL, CP)
    own = jnp.where(jnp.arange(CP) < CL, own, NONE)
    have = jnp.bitwise_xor(own[:, None], occ_irrep[None, :]).reshape(1, CP * O)
    high, low = fold(occ_irrep, vir_row, have, cycle_weight.T)
    fits, slots = lax.optimization_barrier((fits[0, 0] > 0.5, slots))

    partial = contract(received, slots, valid, rank, high, low)
    near = lax.ppermute(partial[1:3], "grp", [(d, d ^ 1) for d in range(G)])
    mine = partial[0] + near[0]
    last = lax.ppermute(partial[3] + near[1], "grp", [(d, d ^ 3) for d in range(G)])
    return finish(mine, last, pick, keep, divisor).T, fits


def plain_form(amplitudes, cycle_weight, occ_irrep, vir_irrep, occ_energy, vir_energy):
    g = lax.axis_index("grp")
    m = lax.axis_index("blk")
    own = lax.dynamic_slice_in_dim(vir_irrep, g * CL, CL)
    own_b = lax.dynamic_slice_in_dim(vir_irrep, m * BL, BL)
    sent = jnp.transpose(amplitudes.reshape(T * CL, BW)).reshape(M, BL, T * CL)
    received = lax.all_to_all(sent, "blk", 0, 0, tiled=True)
    amp = jnp.transpose(received.reshape(M, BL, T, CL), (0, 2, 1, 3)).reshape(O, O, BL, CL)
    pairs = jnp.bitwise_xor(occ_irrep[:, None], occ_irrep[None, :])
    allowed = jnp.bitwise_xor(pairs[:, :, None], own_b)[..., None] == own
    amp = jnp.where(allowed, amp, jnp.zeros_like(amp))
    weight = cycle_weight.reshape(V, CL, O)
    need = jnp.bitwise_xor(vir_irrep, occ_irrep[0])
    have = jnp.bitwise_xor(own[:, None], occ_irrep[None, :])
    weight = jnp.where(need[:, None, None] == have, weight, jnp.zeros_like(weight))
    partial = jnp.einsum("kjbc,xck->xbj", amp, weight, precision=HIGHEST).reshape(G, CL, J4)
    cycle = jnp.sum(lax.all_to_all(partial, "grp", 0, 0, tiled=True).reshape(G, CL, J4), axis=0)
    row_energy = occ_energy[0] - lax.dynamic_slice_in_dim(vir_energy, g * CL, CL)
    slab_energy = lax.dynamic_slice_in_dim(vir_energy, m * BL, BL)
    col_energy = (occ_energy[None, :] - slab_energy[:, None]).reshape(J4)
    return cycle / (row_energy[:, None] + col_energy[None, :])


def shards(*arrays):
    out, fits = packed_form(*arrays)
    return lax.cond(fits, lambda: out, lambda: plain_form(*arrays))


def solution(mesh):
    in_specs = (P("blk", "grp", None), P(None, "grp"), P(), P(), P(), P())
    out_specs = P("grp", "blk")
    return jax.shard_map(shards, mesh=mesh, in_specs=in_specs, out_specs=out_specs, check_vma=False)
```

```python
import jax
import jax.numpy as jnp
from jax import lax
from jax.experimental import pallas as pl
from jax.experimental.pallas import tpu as pltpu
from jax.sharding import PartitionSpec as P

O = 40
V = 500
IW = 1
BW = 256
G = 4
M = 64
CL = V // G
CP = 128
T = O * O // M
TS = 5
BL = BW // M
J4 = O * BL
SLOTS = 640
FOLD = 40
NF = G * FOLD
GT = 3
NG = -(-T // GT)
STEP_SLOTS = ((0, 176), (16, 304), (48, 416), (112, 528), (160, SLOTS))
GROUP_BLOCKS = ((0, 1), (0, 2), (0, 3), (0, 3), (0, 4), (0, 4), (1, 5), (1, 5), (1, 5))
SLOT_FROM = tuple(max(CP * GROUP_BLOCKS[t // GT][0], STEP_SLOTS[t // TS][0]) for t in range(T))
SLOT_TO = tuple(min(CP * GROUP_BLOCKS[t // GT][1], STEP_SLOTS[t // TS][1]) for t in range(T))
NONE = 16

HIGHEST = lax.Precision.HIGHEST
F32 = jnp.float32
BF16 = jnp.bfloat16
I32 = jnp.int32


def dot(a, b):
    return jnp.dot(a, b, preferred_element_type=F32)


def halves(x):
    high = x.astype(BF16)
    return high, (x - high.astype(F32)).astype(BF16)


def in_hbm(x):
    return pltpu.with_memory_space_constraint(x, pltpu.HBM)


def share_of(ref, share):
    first = share * CL
    over = first - (V - CP)
    if over <= 0:
        return ref[:, first : first + CP]
    return pltpu.roll(ref[:, V - CP : V], CP - over, 1)


def own_share(ref, g):
    row = share_of(ref, 0)
    for share in range(1, G):
        row = jnp.where(g == share, share_of(ref, share), row)
    return row


def labels_of(row):
    return jnp.where(iota((1, CP), 1) < CL, row, NONE)


def same_before(row):
    wide = jnp.broadcast_to(row, (CP, CP))
    return ((wide == jnp.transpose(wide)) & (iota((CP, CP), 0) < iota((CP, CP), 1))).astype(F32)


def one_hot(x):
    return x.astype(F32).astype(BF16)


def iota(shape, dim):
    return lax.broadcasted_iota(I32, shape, dim)


def pack_kernel(occ_ref, vir_ref, amp_ref, out_ref, rank_ref, column_ref, count_ref, base_ref, total_ref, pick_ref, both_ref):
    step = pl.program_id(0)
    g = lax.axis_index("grp")
    m = lax.axis_index("blk")
    row = vir_ref[:, 0:CP]
    for other in range(1, G):
        row = jnp.where(g == other, vir_ref[:, other * CL : other * CL + CP], row)
    row = jnp.where(iota((1, CP), 1) < CL, row, NONE)

    @pl.when(step == 0)
    def _():
        wide = jnp.broadcast_to(row, (CP, CP))
        column = jnp.transpose(wide)
        column_ref[...] = column
        before = (wide == column) & (iota((CP, CP), 0) < iota((CP, CP), 1))
        rank_ref[...] = jnp.sum(before.astype(F32), axis=0, keepdims=True).astype(I32)
        for q in range(8):
            same = (iota((8, CP), 0) == jnp.bitwise_xor(row, q)).astype(F32)
            count_ref[q] = jnp.broadcast_to(jnp.sum(same, axis=1, keepdims=True), (8, CP)).astype(I32)
        base_ref[...] = jnp.zeros_like(base_ref)
        total_ref[...] = jnp.zeros_like(total_ref)

    for phase, (first, last) in enumerate(STEP_SLOTS):

        @pl.when(step == phase)
        def _():
            for t in range(TS):
                pair = m * T + phase * TS + t
                q = jnp.bitwise_xor(occ_ref[pair // O], occ_ref[pair % O])
                same = iota((8, CP), 0) == jnp.bitwise_xor(row, q)
                base = jnp.sum(jnp.where(same, base_ref[...], 0).astype(F32), axis=0, keepdims=True).astype(I32)
                slot = base + rank_ref[...] - first
                base_ref[...] += count_ref[q]
                columns = slice(t * CP, (t + 1) * CP)
                pick_ref[0 : last - first, columns] = (iota((last - first, CP), 0) == slot).astype(F32).astype(BF16)
                need = jnp.bitwise_xor(column_ref[...], q)
                for half in range(BW // CP):
                    lanes = slice(half * CP, (half + 1) * CP)
                    block = jnp.where(need == vir_ref[:, lanes], amp_ref[t, :, lanes], 0.0)
                    high, low = halves(block)
                    both_ref[columns, lanes] = high
                    both_ref[TS * CP + t * CP : TS * CP + (t + 1) * CP, lanes] = low
            pick = pick_ref[0 : last - first]
            total_ref[first:last] += dot(jnp.concatenate([pick, pick], axis=1), both_ref[...])

    @pl.when(step == pl.num_programs(0) - 1)
    def _():
        out_ref[...] = jnp.transpose(total_ref[...]).reshape(M, BL, SLOTS)


def pack(occ_irrep, vir_row, amplitudes):
    return pl.pallas_call(
        pack_kernel,
        name="pack_amplitudes",
        grid=(T // TS,),
        out_shape=jax.ShapeDtypeStruct((M, BL, SLOTS), F32),
        in_specs=[
            pl.BlockSpec(memory_space=pltpu.SMEM),
            pl.BlockSpec((1, G * CP), lambda s: (0, 0)),
            pl.BlockSpec((TS, CP, BW), lambda s: (s, 0, 0)),
        ],
        out_specs=pl.BlockSpec((M, BL, SLOTS), lambda s: (0, 0, 0)),
        scratch_shapes=[
            pltpu.VMEM((1, CP), I32),
            pltpu.VMEM((CP, CP), I32),
            pltpu.VMEM((8, 8, CP), I32),
            pltpu.VMEM((8, CP), I32),
            pltpu.VMEM((SLOTS, BW), F32),
            pltpu.VMEM((SLOTS, TS * CP), BF16),
            pltpu.VMEM((2 * TS * CP, BW), BF16),
        ],
        compiler_params=pltpu.CompilerParams(vmem_limit_bytes=8 << 20),
    )(occ_irrep, vir_row, amplitudes)


CS = 16


def fold_kernel(
    occ_ref, vir_ref, have_ref, w_ref, high_ref, low_ref, lay_ref, pick_ref, turn_ref, rest_ref, first_ref, second_ref
):
    step = pl.program_id(0)

    @pl.when(step == 0)
    def _():
        for share in range(G):
            before = jnp.transpose(same_before(labels_of(share_of(vir_ref, share))))
            rank = jnp.sum(before, axis=1, keepdims=True).astype(I32)
            hit = (iota((CP, NF), 1) == rank + share * FOLD) & (rank < FOLD)
            lay_ref[share * CL : share * CL + CP, :] = hit.astype(F32)
        pick_ref[...] = lay_ref[...].astype(BF16)

    need = jnp.bitwise_xor(vir_ref[...], occ_ref[0])
    for part in range(CS * O // CP):
        rows = slice(part * CP, (part + 1) * CP)
        have = jnp.transpose(jnp.broadcast_to(have_ref[:, rows], (CP, CP)))
        for first in range(0, V, CP):
            lanes = slice(first, min(first + CP, V))
            kept = jnp.where(need[:, lanes] == have[:, : min(CP, V - first)], w_ref[rows, lanes], 0.0)
            high, low = halves(kept)
            first_ref[rows, lanes] = high
            second_ref[rows, lanes] = low
    folded = dot(first_ref[...], pick_ref[0:V]) + dot(second_ref[...], pick_ref[0:V])
    turn_ref[...] = folded[:, 0:CP]
    rest_ref[:, 0 : NF - CP] = folded[:, CP:NF]
    for k in range(O):
        rows = pl.ds(k, CS, stride=O)
        part = jnp.concatenate([turn_ref[rows, :], rest_ref[rows, :]], axis=1)
        high, low = halves(part[:, 0:NF])
        high_ref[k] = high
        low_ref[k] = low


def fold(occ_irrep, vir_row, have, turned_weight):
    rows = CS * O
    out = pltpu.HBM((O, CP, NF), BF16)
    spec = pl.BlockSpec((O, CS, NF), lambda s: (0, s, 0))
    return pl.pallas_call(
        fold_kernel,
        name="fold_weights",
        grid=(CP // CS,),
        out_shape=(out, out),
        in_specs=[
            pl.BlockSpec(memory_space=pltpu.SMEM),
            pl.BlockSpec((1, V), lambda s: (0, 0)),
            pl.BlockSpec((1, rows), lambda s: (0, s)),
            pl.BlockSpec((rows, V), lambda s: (s, 0)),
        ],
        out_specs=(spec, spec),
        scratch_shapes=[pltpu.VMEM((G * CP, NF), F32), pltpu.VMEM((G * CP, NF), BF16), pltpu.VMEM((rows, CP), F32), pltpu.VMEM((rows, CP), F32)]
        + [pltpu.VMEM((rows, V), BF16)] * 2,
        compiler_params=pltpu.CompilerParams(vmem_limit_bytes=8 << 20),
    )(occ_irrep, vir_row, have, turned_weight)


def amounts(kinds, counts):
    found = jnp.zeros(kinds.shape, I32)
    for label in range(8):
        found = jnp.where(kinds == label, counts[label], found)
    return one_hot(found)


def table_kernel(
    occ_ref, vir_ref, occ_energy_ref, vir_energy_ref, vir_row_ref, energy_row_ref, from_ref, to_ref,
    slot_ref, valid_ref, fits_ref, rank_ref, pick_ref, keep_ref, divisor_ref,
):
    g = lax.axis_index("grp")
    m = lax.axis_index("blk")
    own = labels_of(own_share(vir_row_ref, g))
    rank = jnp.sum(same_before(own), axis=0, keepdims=True).astype(I32)
    rank_ref[...] = rank
    pick_ref[...] = (iota((FOLD, CP), 0) == rank).astype(F32)

    counts = []
    for share in range(G):
        row = labels_of(share_of(vir_row_ref, share))
        counts.append([jnp.sum((row == label).astype(F32), axis=1, keepdims=True).astype(I32) for label in range(8)])
    held = counts[0]
    for share in range(1, G):
        held = [jnp.where(g == share, new, old) for new, old in zip(counts[share], held)]

    number = iota((M, T), 0) * T + iota((M, T), 1)
    k, j = number // O, number % O
    kind_k, kind_j = jnp.zeros((M, T), I32), jnp.zeros((M, T), I32)
    for o in range(O):
        kind_k = jnp.where(k == o, occ_ref[o], kind_k)
        kind_j = jnp.where(j == o, occ_ref[o], kind_j)
    kinds = one_hot(jnp.bitwise_xor(kind_k, kind_j))
    rows = iota((M * BL, 1), 0)
    label = jnp.zeros((M * BL, 1), I32)
    for b in range(BL):
        label = jnp.where(rows % BL == b, vir_ref[m * BL + b], label)
    mine = dot(one_hot(iota((M * BL, M), 0) // BL == iota((M * BL, M), 1)), kinds).astype(I32)
    mine = jnp.bitwise_xor(mine, label)
    every = dot(one_hot(iota((M * 8, M), 0) // 8 == iota((M * 8, M), 1)), kinds).astype(I32)
    every = jnp.bitwise_xor(every, iota((M * 8, 1), 0) % 8)

    amount_of = amounts(mine, held)
    pair = iota((T, CP), 0)
    at = iota((T, CP), 1) // FOLD
    place = iota((M * BL, CP), 1) % FOLD
    real = iota((M * BL, CP), 1) < GT * FOLD
    for group in range(NG):
        start = dot(amount_of, one_hot(pair < GT * group + at)).astype(I32)
        amount = dot(amount_of, one_hot(pair == GT * group + at)).astype(I32)
        slot_ref[group] = jnp.where(real & (place < amount), start + place, -1)
    mine = one_hot(mine)
    for t in range(T):
        valid_ref[t] = (dot(mine, one_hot(pair == t)).astype(I32) == own).astype(F32)

    most = counts[0][0]
    for share in range(G):
        for count in counts[share]:
            most = jnp.maximum(most, count)
    good = jnp.ones((8 * M, T), F32)
    earlier = one_hot(iota((T, T), 0) < iota((T, T), 1))
    for share in range(G):
        start = dot(amounts(every, counts[share]), earlier).astype(I32)
        good = jnp.where((start >= from_ref[...]) & (start + most <= to_ref[...]), good, 0.0)
    fits = jnp.where(most <= FOLD, jnp.min(good, axis=(0, 1), keepdims=True), 0.0)
    fits_ref[...] = jnp.broadcast_to(fits, (8, CP))

    row = iota((J4, CP), 0)
    occ_label, occ_energy = jnp.zeros((J4, CP), I32), jnp.zeros((J4, CP), F32)
    for o in range(O):
        occ_label = jnp.where(row % O == o, occ_ref[o], occ_label)
        occ_energy = jnp.where(row % O == o, occ_energy_ref[o], occ_energy)
    vir_label, vir_energy = jnp.zeros((J4, CP), I32), jnp.zeros((J4, CP), F32)
    for b in range(BL):
        vir_label = jnp.where(row // O == b, vir_ref[m * BL + b], vir_label)
        vir_energy = jnp.where(row // O == b, vir_energy_ref[m * BL + b], vir_energy)
    need = jnp.bitwise_xor(own, occ_ref[0])
    keep_ref[...] = (need == jnp.bitwise_xor(occ_label, vir_label)).astype(F32)
    row_energy = occ_energy_ref[0] - own_share(energy_row_ref, g)
    divisor_ref[...] = row_energy + (occ_energy - vir_energy)


def tables(occ_irrep, vir_irrep, occ_energy, vir_energy):
    smem = pl.BlockSpec(memory_space=pltpu.SMEM)
    vmem = pl.BlockSpec(memory_space=pltpu.VMEM)
    low, high = (jnp.array(x, I32).reshape(1, T) for x in (SLOT_FROM, SLOT_TO))
    return pl.pallas_call(
        table_kernel,
        name="tables",
        out_shape=(
            pltpu.HBM((NG, M * BL, CP), I32),
            jax.ShapeDtypeStruct((T, M * BL, CP), F32),
            jax.ShapeDtypeStruct((8, CP), F32),
            jax.ShapeDtypeStruct((1, CP), I32),
            jax.ShapeDtypeStruct((FOLD, CP), F32),
            jax.ShapeDtypeStruct((J4, CP), F32),
            jax.ShapeDtypeStruct((J4, CP), F32),
        ),
        in_specs=[smem] * 4 + [vmem] * 4,
        compiler_params=pltpu.CompilerParams(vmem_limit_bytes=8 << 20),
    )(occ_irrep, vir_irrep, occ_energy, vir_energy, vir_irrep.reshape(1, V), vir_energy.reshape(1, V), low, high)


REST = J4 - CP
DENSE = FOLD + 16


def to_lanes(x):
    rest = [x[at : at + 8, CP:J4] for at in range(0, FOLD, 8)]
    tail = jnp.concatenate(rest[4:] + [jnp.zeros((8, CP - REST), F32)], axis=1)
    return jnp.concatenate([x[:, 0:CP], jnp.concatenate(rest[:4], axis=1), tail], axis=0)


def from_lanes(x):
    rest = [x[FOLD : FOLD + 8, at * REST : (at + 1) * REST] for at in range(4)] + [x[FOLD + 8 : DENSE, 0:REST]]
    return jnp.concatenate([x[0:FOLD], jnp.concatenate(rest, axis=0)], axis=1)


def contract_kernel(
    far_x_ref, far_slot_ref, valid_ref, rank_ref, far_high_ref, far_low_ref, out_ref,
    x_ref, slot_ref, seen_ref, spread_ref, wide_ref, high_ref, low_ref, sem,
):
    g = lax.axis_index("grp")
    quarter = M // 4
    x_copies, slot_copies = [], []
    for part in range(4):
        x_rows = pl.ds(part * quarter, quarter)
        slot_rows = pl.ds(part * quarter * BL, quarter * BL)
        x_copies.append(pltpu.make_async_copy(far_x_ref.at[x_rows], x_ref.at[x_rows], sem.at[2 + part]))
        slot_copies.append(
            pltpu.make_async_copy(far_slot_ref.at[:, slot_rows], slot_ref.at[:, slot_rows], sem.at[6 + part])
        )
        x_copies[part].start()
        slot_copies[part].start()
    copies = [
        pltpu.make_async_copy(far_high_ref, high_ref, sem.at[0]),
        pltpu.make_async_copy(far_low_ref, low_ref, sem.at[1]),
    ]
    for copy in copies:
        copy.start()

    for quarter_at in range(4):
        x_copies[quarter_at].wait()
        slot_copies[quarter_at].wait()

        @pl.loop(quarter_at * 2, quarter_at * 2 + 2)
        def _(i):
            for near in range(4):
                packed = x_ref[pl.ds(8 * i + 2 * near, 2)].reshape(2 * BL, SLOTS)
                rows = pl.ds(pl.multiple_of(32 * i, 8) + 8 * near, 8)
                for group, (first, last) in enumerate(GROUP_BLOCKS):
                    slot = slot_ref[group, rows, :]
                    lane = jnp.bitwise_and(slot, CP - 1)
                    where = jnp.right_shift(slot, 7)
                    found = jnp.zeros((8, CP), F32)
                    for part in range(first, last):
                        taken = jnp.take_along_axis(
                            packed[:, part * CP : (part + 1) * CP], lane, axis=1, mode="promise_in_bounds"
                        )
                        found = jnp.where(where == part, taken, found)
                    seen_ref[group, rows, :] = found

    place = [(iota((CP, CP), 0) - at * FOLD == rank_ref[...]).astype(F32).astype(BF16) for at in range(GT)]
    place = jnp.concatenate(place, axis=1)
    place = jnp.concatenate([place, place], axis=0)
    for group in range(NG):
        spread_ref[group] = dot(jnp.concatenate(halves(seen_ref[group]), axis=1), place)

    @pl.loop(0, M // 2)
    def _(i):
        rows = pl.ds(pl.multiple_of(8 * i, 8), 8)
        first = pl.multiple_of(2 * T * BL * i, 8)
        for t in range(T):
            at = (t % GT) * CP
            row = spread_ref[t // GT, rows, at : at + CP] * valid_ref[t, rows, :]
            if t % 2 == 0:
                one, two = row[0:BL], row[BL : 2 * BL]
            else:
                row = pltpu.roll(row, BL, 0)
                one, two = row[BL : 2 * BL], row[0:BL]
            wide_ref[pl.ds(first + BL * t, BL), :] = one
            wide_ref[pl.ds(first + T * BL + BL * t, BL), :] = two

    for copy in copies:
        copy.wait()
    total = jnp.zeros((J4, NF), F32)
    for i in range(O // 2):
        first = 2 * J4 * i
        amp = jnp.concatenate([wide_ref[first : first + J4], wide_ref[first + J4 : first + 2 * J4]], axis=1)
        a_high, a_low = halves(amp)
        w_high = high_ref[2 * i : 2 * i + 2].reshape(2 * CP, NF)
        w_low = low_ref[2 * i : 2 * i + 2].reshape(2 * CP, NF)
        both = dot(jnp.concatenate([a_high, a_low], axis=0), w_high)
        total = total + (both[0:J4] + both[J4 : 2 * J4] + dot(a_high, w_low))

    turned = jnp.transpose(total)
    for block in range(G):
        part = turned[block * FOLD : (block + 1) * FOLD]
        out_ref[jnp.bitwise_xor(g, block)] = to_lanes(part)


def contract(received, slots, valid, rank, high, low):
    vmem = pl.BlockSpec(memory_space=pltpu.VMEM)
    hbm = pl.BlockSpec(memory_space=pltpu.HBM)
    return pl.pallas_call(
        contract_kernel,
        name="contract",
        out_shape=jax.ShapeDtypeStruct((G, DENSE, CP), F32),
        in_specs=[hbm, hbm, vmem, vmem, hbm, hbm],
        scratch_shapes=[
            pltpu.VMEM((M, BL, SLOTS), F32),
            pltpu.VMEM((NG, M * BL, CP), I32),
            pltpu.VMEM((NG, M * BL, CP), F32),
            pltpu.VMEM((NG, M * BL, GT * CP), F32),
            pltpu.VMEM((O * O * BL, CP), F32),
            pltpu.VMEM((O, CP, NF), BF16),
            pltpu.VMEM((O, CP, NF), BF16),
            pltpu.SemaphoreType.DMA((10,)),
        ],
        compiler_params=pltpu.CompilerParams(vmem_limit_bytes=20 << 20),
    )(in_hbm(received), in_hbm(slots), valid, rank, in_hbm(high), in_hbm(low))


def finish_kernel(a_ref, b_ref, pick_ref, keep_ref, divisor_ref, out_ref):
    folded = from_lanes(a_ref[...] + b_ref[...])
    source = iota((J4, J4), 0)
    target = iota((J4, J4), 1)
    move = (source % BL) * O + source // BL == target
    high, low = halves(folded)
    folded = dot(high, one_hot(move)) + dot(low, one_hot(move))
    high, low = halves(jnp.transpose(folded))
    pick = pick_ref[...].astype(BF16)
    wide = dot(high, pick) + dot(low, pick)
    wide = jnp.where(keep_ref[...] > 0, wide, 0.0) / divisor_ref[...]
    out_ref[...] = wide[:, 0:CL]


def finish(a, b, pick, keep, divisor):
    return pl.pallas_call(
        finish_kernel,
        name="finish",
        out_shape=pltpu.HBM((J4, CL), F32),
        compiler_params=pltpu.CompilerParams(vmem_limit_bytes=4 << 20),
    )(a, b, pick, keep, divisor)


def packed_form(amplitudes, cycle_weight, occ_irrep, vir_irrep, occ_energy, vir_energy):
    g = lax.axis_index("grp")
    vir_row = vir_irrep.reshape(1, V)
    sent = pack(occ_irrep, vir_row, amplitudes)
    received = lax.all_to_all(sent, "blk", 0, 0, tiled=True)

    slots, valid, fits, rank, pick, keep, divisor = tables(occ_irrep, vir_irrep, occ_energy, vir_energy)
    own = lax.dynamic_slice_in_dim(jnp.pad(vir_irrep, (0, CP - CL)), g * CL, CP)
    own = jnp.where(jnp.arange(CP) < CL, own, NONE)
    have = jnp.bitwise_xor(own[:, None], occ_irrep[None, :]).reshape(1, CP * O)
    high, low = fold(occ_irrep, vir_row, have, cycle_weight.T)
    fits, slots = lax.optimization_barrier((fits[0, 0] > 0.5, slots))

    partial = contract(received, slots, valid, rank, high, low)
    near = lax.ppermute(partial[1:3], "grp", [(d, d ^ 1) for d in range(G)])
    mine = partial[0] + near[0]
    last = lax.ppermute(partial[3] + near[1], "grp", [(d, d ^ 3) for d in range(G)])
    return finish(mine, last, pick, keep, divisor).T, fits


def plain_form(amplitudes, cycle_weight, occ_irrep, vir_irrep, occ_energy, vir_energy):
    g = lax.axis_index("grp")
    m = lax.axis_index("blk")
    own = lax.dynamic_slice_in_dim(vir_irrep, g * CL, CL)
    own_b = lax.dynamic_slice_in_dim(vir_irrep, m * BL, BL)
    sent = jnp.transpose(amplitudes.reshape(T * CL, BW)).reshape(M, BL, T * CL)
    received = lax.all_to_all(sent, "blk", 0, 0, tiled=True)
    amp = jnp.transpose(received.reshape(M, BL, T, CL), (0, 2, 1, 3)).reshape(O, O, BL, CL)
    pairs = jnp.bitwise_xor(occ_irrep[:, None], occ_irrep[None, :])
    allowed = jnp.bitwise_xor(pairs[:, :, None], own_b)[..., None] == own
    amp = jnp.where(allowed, amp, jnp.zeros_like(amp))
    weight = cycle_weight.reshape(V, CL, O)
    need = jnp.bitwise_xor(vir_irrep, occ_irrep[0])
    have = jnp.bitwise_xor(own[:, None], occ_irrep[None, :])
    weight = jnp.where(need[:, None, None] == have, weight, jnp.zeros_like(weight))
    partial = jnp.einsum("kjbc,xck->xbj", amp, weight, precision=HIGHEST).reshape(G, CL, J4)
    cycle = jnp.sum(lax.all_to_all(partial, "grp", 0, 0, tiled=True).reshape(G, CL, J4), axis=0)
    row_energy = occ_energy[0] - lax.dynamic_slice_in_dim(vir_energy, g * CL, CL)
    slab_energy = lax.dynamic_slice_in_dim(vir_energy, m * BL, BL)
    col_energy = (occ_energy[None, :] - slab_energy[:, None]).reshape(J4)
    return cycle / (row_energy[:, None] + col_energy[None, :])


def shards(*arrays):
    out, fits = packed_form(*arrays)
    return lax.cond(fits, lambda: out, lambda: plain_form(*arrays))


def solution(mesh):
    in_specs = (P("blk", "grp", None), P(None, "grp"), P(), P(), P(), P())
    out_specs = P("grp", "blk")
    return jax.shard_map(shards, mesh=mesh, in_specs=in_specs, out_specs=out_specs, check_vma=False)
```

```python
import jax
import jax.numpy as jnp
from jax import lax
from jax.experimental import pallas as pl
from jax.experimental.pallas import tpu as pltpu
from jax.sharding import PartitionSpec as P

O = 40
V = 500
IW = 1
BW = 256
G = 4
M = 64
CL = V // G
CP = 128
T = O * O // M
TS = 5
BL = BW // M
J4 = O * BL
SLOTS = 640
FOLD = 40
NF = G * FOLD
GT = 3
NG = -(-T // GT)
STEP_SLOTS = ((0, 192), (16, 320), (48, 432), (96, 544), (144, SLOTS))
GROUP_BLOCKS = ((0, 1), (0, 2), (0, 3), (0, 3), (0, 4), (0, 4), (1, 5), (1, 5), (1, 5))
SLOT_FROM = tuple(max(CP * GROUP_BLOCKS[t // GT][0], STEP_SLOTS[t // TS][0]) for t in range(T))
SLOT_TO = tuple(min(CP * GROUP_BLOCKS[t // GT][1], STEP_SLOTS[t // TS][1]) for t in range(T))
NONE = 16

HIGHEST = lax.Precision.HIGHEST
F32 = jnp.float32
BF16 = jnp.bfloat16
I32 = jnp.int32


def dot(a, b):
    return jnp.dot(a, b, preferred_element_type=F32)


def halves(x):
    high = x.astype(BF16)
    return high, (x - high.astype(F32)).astype(BF16)


def in_hbm(x):
    return pltpu.with_memory_space_constraint(x, pltpu.HBM)


def share_of(ref, share):
    first = share * CL
    over = first - (V - CP)
    if over <= 0:
        return ref[:, first : first + CP]
    return pltpu.roll(ref[:, V - CP : V], CP - over, 1)


def own_share(ref, g):
    row = share_of(ref, 0)
    for share in range(1, G):
        row = jnp.where(g == share, share_of(ref, share), row)
    return row


def labels_of(row):
    return jnp.where(iota((1, CP), 1) < CL, row, NONE)


def same_before(row):
    wide = jnp.broadcast_to(row, (CP, CP))
    return ((wide == jnp.transpose(wide)) & (iota((CP, CP), 0) < iota((CP, CP), 1))).astype(F32)


def one_hot(x):
    return x.astype(F32).astype(BF16)


def iota(shape, dim):
    return lax.broadcasted_iota(I32, shape, dim)


def pack_kernel(occ_ref, vir_ref, amp_ref, out_ref, rank_ref, column_ref, count_ref, base_ref, total_ref, pick_ref, both_ref):
    step = pl.program_id(0)
    g = lax.axis_index("grp")
    m = lax.axis_index("blk")
    row = vir_ref[:, 0:CP]
    for other in range(1, G):
        row = jnp.where(g == other, vir_ref[:, other * CL : other * CL + CP], row)
    row = jnp.where(iota((1, CP), 1) < CL, row, NONE)

    @pl.when(step == 0)
    def _():
        wide = jnp.broadcast_to(row, (CP, CP))
        column = jnp.transpose(wide)
        column_ref[...] = column
        before = (wide == column) & (iota((CP, CP), 0) < iota((CP, CP), 1))
        rank_ref[...] = jnp.sum(before.astype(F32), axis=0, keepdims=True).astype(I32)
        for q in range(8):
            same = (iota((8, CP), 0) == jnp.bitwise_xor(row, q)).astype(F32)
            count_ref[q] = jnp.broadcast_to(jnp.sum(same, axis=1, keepdims=True), (8, CP)).astype(I32)
        base_ref[...] = jnp.zeros_like(base_ref)
        total_ref[...] = jnp.zeros_like(total_ref)

    for phase, (first, last) in enumerate(STEP_SLOTS):

        @pl.when(step == phase)
        def _():
            for t in range(TS):
                pair = m * T + phase * TS + t
                q = jnp.bitwise_xor(occ_ref[pair // O], occ_ref[pair % O])
                same = iota((8, CP), 0) == jnp.bitwise_xor(row, q)
                base = jnp.sum(jnp.where(same, base_ref[...], 0).astype(F32), axis=0, keepdims=True).astype(I32)
                slot = base + rank_ref[...] - first
                base_ref[...] += count_ref[q]
                columns = slice(t * CP, (t + 1) * CP)
                pick_ref[0 : last - first, columns] = (iota((last - first, CP), 0) == slot).astype(F32).astype(BF16)
                need = jnp.bitwise_xor(column_ref[...], q)
                for half in range(BW // CP):
                    lanes = slice(half * CP, (half + 1) * CP)
                    block = jnp.where(need == vir_ref[:, lanes], amp_ref[t, :, lanes], 0.0)
                    high, low = halves(block)
                    both_ref[columns, lanes] = high
                    both_ref[TS * CP + t * CP : TS * CP + (t + 1) * CP, lanes] = low
            pick = pick_ref[0 : last - first]
            total_ref[first:last] += dot(jnp.concatenate([pick, pick], axis=1), both_ref[...])

    @pl.when(step == pl.num_programs(0) - 1)
    def _():
        out_ref[...] = jnp.transpose(total_ref[...]).reshape(M, BL, SLOTS)


def pack(occ_irrep, vir_row, amplitudes):
    return pl.pallas_call(
        pack_kernel,
        name="pack_amplitudes",
        grid=(T // TS,),
        out_shape=jax.ShapeDtypeStruct((M, BL, SLOTS), F32),
        in_specs=[
            pl.BlockSpec(memory_space=pltpu.SMEM),
            pl.BlockSpec((1, G * CP), lambda s: (0, 0)),
            pl.BlockSpec((TS, CP, BW), lambda s: (s, 0, 0)),
        ],
        out_specs=pl.BlockSpec((M, BL, SLOTS), lambda s: (0, 0, 0)),
        scratch_shapes=[
            pltpu.VMEM((1, CP), I32),
            pltpu.VMEM((CP, CP), I32),
            pltpu.VMEM((8, 8, CP), I32),
            pltpu.VMEM((8, CP), I32),
            pltpu.VMEM((SLOTS, BW), F32),
            pltpu.VMEM((SLOTS, TS * CP), BF16),
            pltpu.VMEM((2 * TS * CP, BW), BF16),
        ],
        compiler_params=pltpu.CompilerParams(vmem_limit_bytes=8 << 20),
    )(occ_irrep, vir_row, amplitudes)


CS = 16


def fold_kernel(
    occ_ref, vir_ref, have_ref, w_ref, high_ref, low_ref, lay_ref, pick_ref, turn_ref, rest_ref, first_ref, second_ref
):
    step = pl.program_id(0)

    @pl.when(step == 0)
    def _():
        for share in range(G):
            before = jnp.transpose(same_before(labels_of(share_of(vir_ref, share))))
            rank = jnp.sum(before, axis=1, keepdims=True).astype(I32)
            hit = (iota((CP, NF), 1) == rank + share * FOLD) & (rank < FOLD)
            lay_ref[share * CL : share * CL + CP, :] = hit.astype(F32)
        pick_ref[...] = lay_ref[...].astype(BF16)

    need = jnp.bitwise_xor(vir_ref[...], occ_ref[0])
    for part in range(CS * O // CP):
        rows = slice(part * CP, (part + 1) * CP)
        have = jnp.transpose(jnp.broadcast_to(have_ref[:, rows], (CP, CP)))
        for first in range(0, V, CP):
            lanes = slice(first, min(first + CP, V))
            kept = jnp.where(need[:, lanes] == have[:, : min(CP, V - first)], w_ref[rows, lanes], 0.0)
            high, low = halves(kept)
            first_ref[rows, lanes] = high
            second_ref[rows, lanes] = low
    folded = dot(first_ref[...], pick_ref[0:V]) + dot(second_ref[...], pick_ref[0:V])
    turn_ref[...] = folded[:, 0:CP]
    rest_ref[:, 0 : NF - CP] = folded[:, CP:NF]
    for k in range(O):
        rows = pl.ds(k, CS, stride=O)
        part = jnp.concatenate([turn_ref[rows, :], rest_ref[rows, :]], axis=1)
        high, low = halves(part[:, 0:NF])
        high_ref[k] = high
        low_ref[k] = low


def fold(occ_irrep, vir_row, have, turned_weight):
    rows = CS * O
    out = pltpu.HBM((O, CP, NF), BF16)
    spec = pl.BlockSpec((O, CS, NF), lambda s: (0, s, 0))
    return pl.pallas_call(
        fold_kernel,
        name="fold_weights",
        grid=(CP // CS,),
        out_shape=(out, out),
        in_specs=[
            pl.BlockSpec(memory_space=pltpu.SMEM),
            pl.BlockSpec((1, V), lambda s: (0, 0)),
            pl.BlockSpec((1, rows), lambda s: (0, s)),
            pl.BlockSpec((rows, V), lambda s: (s, 0)),
        ],
        out_specs=(spec, spec),
        scratch_shapes=[pltpu.VMEM((G * CP, NF), F32), pltpu.VMEM((G * CP, NF), BF16), pltpu.VMEM((rows, CP), F32), pltpu.VMEM((rows, CP), F32)]
        + [pltpu.VMEM((rows, V), BF16)] * 2,
        compiler_params=pltpu.CompilerParams(vmem_limit_bytes=8 << 20),
    )(occ_irrep, vir_row, have, turned_weight)


def amounts(kinds, counts):
    found = jnp.zeros(kinds.shape, I32)
    for label in range(8):
        found = jnp.where(kinds == label, counts[label], found)
    return one_hot(found)


def table_kernel(
    occ_ref, vir_ref, occ_energy_ref, vir_energy_ref, vir_row_ref, energy_row_ref, from_ref, to_ref,
    slot_ref, valid_ref, fits_ref, rank_ref, pick_ref, keep_ref, divisor_ref,
):
    g = lax.axis_index("grp")
    m = lax.axis_index("blk")
    own = labels_of(own_share(vir_row_ref, g))
    rank = jnp.sum(same_before(own), axis=0, keepdims=True).astype(I32)
    rank_ref[...] = rank
    pick_ref[...] = (iota((FOLD, CP), 0) == rank).astype(F32)

    counts = []
    for share in range(G):
        row = labels_of(share_of(vir_row_ref, share))
        counts.append([jnp.sum((row == label).astype(F32), axis=1, keepdims=True).astype(I32) for label in range(8)])
    held = counts[0]
    for share in range(1, G):
        held = [jnp.where(g == share, new, old) for new, old in zip(counts[share], held)]

    number = iota((M, T), 0) * T + iota((M, T), 1)
    k, j = number // O, number % O
    kind_k, kind_j = jnp.zeros((M, T), I32), jnp.zeros((M, T), I32)
    for o in range(O):
        kind_k = jnp.where(k == o, occ_ref[o], kind_k)
        kind_j = jnp.where(j == o, occ_ref[o], kind_j)
    kinds = one_hot(jnp.bitwise_xor(kind_k, kind_j))
    rows = iota((M * BL, 1), 0)
    label = jnp.zeros((M * BL, 1), I32)
    for b in range(BL):
        label = jnp.where(rows % BL == b, vir_ref[m * BL + b], label)
    mine = dot(one_hot(iota((M * BL, M), 0) // BL == iota((M * BL, M), 1)), kinds).astype(I32)
    mine = jnp.bitwise_xor(mine, label)
    every = dot(one_hot(iota((M * 8, M), 0) // 8 == iota((M * 8, M), 1)), kinds).astype(I32)
    every = jnp.bitwise_xor(every, iota((M * 8, 1), 0) % 8)

    amount_of = amounts(mine, held)
    pair = iota((T, CP), 0)
    at = iota((T, CP), 1) // FOLD
    place = iota((M * BL, CP), 1) % FOLD
    real = iota((M * BL, CP), 1) < GT * FOLD
    for group in range(NG):
        start = dot(amount_of, one_hot(pair < GT * group + at)).astype(I32)
        amount = dot(amount_of, one_hot(pair == GT * group + at)).astype(I32)
        slot_ref[group] = jnp.where(real & (place < amount), start + place, -1)
    mine = one_hot(mine)
    for t in range(T):
        valid_ref[t] = (dot(mine, one_hot(pair == t)).astype(I32) == own).astype(F32)

    most = counts[0][0]
    for share in range(G):
        for count in counts[share]:
            most = jnp.maximum(most, count)
    good = jnp.ones((8 * M, T), F32)
    earlier = one_hot(iota((T, T), 0) < iota((T, T), 1))
    for share in range(G):
        start = dot(amounts(every, counts[share]), earlier).astype(I32)
        good = jnp.where((start >= from_ref[...]) & (start + most <= to_ref[...]), good, 0.0)
    fits = jnp.where(most <= FOLD, jnp.min(good, axis=(0, 1), keepdims=True), 0.0)
    fits_ref[...] = jnp.broadcast_to(fits, (8, CP))

    row = iota((J4, CP), 0)
    occ_label, occ_energy = jnp.zeros((J4, CP), I32), jnp.zeros((J4, CP), F32)
    for o in range(O):
        occ_label = jnp.where(row % O == o, occ_ref[o], occ_label)
        occ_energy = jnp.where(row % O == o, occ_energy_ref[o], occ_energy)
    vir_label, vir_energy = jnp.zeros((J4, CP), I32), jnp.zeros((J4, CP), F32)
    for b in range(BL):
        vir_label = jnp.where(row // O == b, vir_ref[m * BL + b], vir_label)
        vir_energy = jnp.where(row // O == b, vir_energy_ref[m * BL + b], vir_energy)
    need = jnp.bitwise_xor(own, occ_ref[0])
    keep_ref[...] = (need == jnp.bitwise_xor(occ_label, vir_label)).astype(F32)
    row_energy = occ_energy_ref[0] - own_share(energy_row_ref, g)
    divisor_ref[...] = row_energy + (occ_energy - vir_energy)


def tables(occ_irrep, vir_irrep, occ_energy, vir_energy):
    smem = pl.BlockSpec(memory_space=pltpu.SMEM)
    vmem = pl.BlockSpec(memory_space=pltpu.VMEM)
    low, high = (jnp.array(x, I32).reshape(1, T) for x in (SLOT_FROM, SLOT_TO))
    return pl.pallas_call(
        table_kernel,
        name="tables",
        out_shape=(
            pltpu.HBM((NG, M * BL, CP), I32),
            jax.ShapeDtypeStruct((T, M * BL, CP), F32),
            jax.ShapeDtypeStruct((8, CP), F32),
            jax.ShapeDtypeStruct((1, CP), I32),
            jax.ShapeDtypeStruct((FOLD, CP), F32),
            jax.ShapeDtypeStruct((J4, CP), F32),
            jax.ShapeDtypeStruct((J4, CP), F32),
        ),
        in_specs=[smem] * 4 + [vmem] * 4,
        compiler_params=pltpu.CompilerParams(vmem_limit_bytes=8 << 20),
    )(occ_irrep, vir_irrep, occ_energy, vir_energy, vir_irrep.reshape(1, V), vir_energy.reshape(1, V), low, high)


REST = J4 - CP
DENSE = FOLD + 16


def to_lanes(x):
    rest = [x[at : at + 8, CP:J4] for at in range(0, FOLD, 8)]
    tail = jnp.concatenate(rest[4:] + [jnp.zeros((8, CP - REST), F32)], axis=1)
    return jnp.concatenate([x[:, 0:CP], jnp.concatenate(rest[:4], axis=1), tail], axis=0)


def from_lanes(x):
    rest = [x[FOLD : FOLD + 8, at * REST : (at + 1) * REST] for at in range(4)] + [x[FOLD + 8 : DENSE, 0:REST]]
    return jnp.concatenate([x[0:FOLD], jnp.concatenate(rest, axis=0)], axis=1)


def contract_kernel(
    far_x_ref, far_slot_ref, valid_ref, rank_ref, far_high_ref, far_low_ref, out_ref,
    x_ref, slot_ref, seen_ref, spread_ref, wide_ref, high_ref, low_ref, sem,
):
    g = lax.axis_index("grp")
    quarter = M // 4
    x_copies, slot_copies = [], []
    for part in range(4):
        x_rows = pl.ds(part * quarter, quarter)
        slot_rows = pl.ds(part * quarter * BL, quarter * BL)
        x_copies.append(pltpu.make_async_copy(far_x_ref.at[x_rows], x_ref.at[x_rows], sem.at[2 + part]))
        slot_copies.append(
            pltpu.make_async_copy(far_slot_ref.at[:, slot_rows], slot_ref.at[:, slot_rows], sem.at[6 + part])
        )
        x_copies[part].start()
        slot_copies[part].start()
    copies = [
        pltpu.make_async_copy(far_high_ref, high_ref, sem.at[0]),
        pltpu.make_async_copy(far_low_ref, low_ref, sem.at[1]),
    ]
    for copy in copies:
        copy.start()

    for quarter_at in range(4):
        x_copies[quarter_at].wait()
        slot_copies[quarter_at].wait()

        @pl.loop(quarter_at * 2, quarter_at * 2 + 2)
        def _(i):
            for near in range(4):
                packed = x_ref[pl.ds(8 * i + 2 * near, 2)].reshape(2 * BL, SLOTS)
                rows = pl.ds(pl.multiple_of(32 * i, 8) + 8 * near, 8)
                for group, (first, last) in enumerate(GROUP_BLOCKS):
                    slot = slot_ref[group, rows, :]
                    lane = jnp.bitwise_and(slot, CP - 1)
                    where = jnp.right_shift(slot, 7)
                    found = jnp.zeros((8, CP), F32)
                    for part in range(first, last):
                        taken = jnp.take_along_axis(
                            packed[:, part * CP : (part + 1) * CP], lane, axis=1, mode="promise_in_bounds"
                        )
                        found = jnp.where(where == part, taken, found)
                    seen_ref[group, rows, :] = found

    place = [(iota((CP, CP), 0) - at * FOLD == rank_ref[...]).astype(F32).astype(BF16) for at in range(GT)]
    place = jnp.concatenate(place, axis=1)
    place = jnp.concatenate([place, place], axis=0)
    for group in range(NG):
        spread_ref[group] = dot(jnp.concatenate(halves(seen_ref[group]), axis=1), place)

    @pl.loop(0, M // 2)
    def _(i):
        rows = pl.ds(pl.multiple_of(8 * i, 8), 8)
        first = pl.multiple_of(2 * T * BL * i, 8)
        for t in range(T):
            at = (t % GT) * CP
            row = spread_ref[t // GT, rows, at : at + CP] * valid_ref[t, rows, :]
            if t % 2 == 0:
                one, two = row[0:BL], row[BL : 2 * BL]
            else:
                row = pltpu.roll(row, BL, 0)
                one, two = row[BL : 2 * BL], row[0:BL]
            wide_ref[pl.ds(first + BL * t, BL), :] = one
            wide_ref[pl.ds(first + T * BL + BL * t, BL), :] = two

    for copy in copies:
        copy.wait()
    total = jnp.zeros((J4, NF), F32)
    for i in range(O // 2):
        first = 2 * J4 * i
        amp = jnp.concatenate([wide_ref[first : first + J4], wide_ref[first + J4 : first + 2 * J4]], axis=1)
        a_high, a_low = halves(amp)
        w_high = high_ref[2 * i : 2 * i + 2].reshape(2 * CP, NF)
        w_low = low_ref[2 * i : 2 * i + 2].reshape(2 * CP, NF)
        both = dot(jnp.concatenate([a_high, a_low], axis=0), w_high)
        total = total + (both[0:J4] + both[J4 : 2 * J4] + dot(a_high, w_low))

    turned = jnp.transpose(total)
    for block in range(G):
        part = turned[block * FOLD : (block + 1) * FOLD]
        out_ref[jnp.bitwise_xor(g, block)] = to_lanes(part)


def contract(received, slots, valid, rank, high, low):
    vmem = pl.BlockSpec(memory_space=pltpu.VMEM)
    hbm = pl.BlockSpec(memory_space=pltpu.HBM)
    return pl.pallas_call(
        contract_kernel,
        name="contract",
        out_shape=jax.ShapeDtypeStruct((G, DENSE, CP), F32),
        in_specs=[hbm, hbm, vmem, vmem, hbm, hbm],
        scratch_shapes=[
            pltpu.VMEM((M, BL, SLOTS), F32),
            pltpu.VMEM((NG, M * BL, CP), I32),
            pltpu.VMEM((NG, M * BL, CP), F32),
            pltpu.VMEM((NG, M * BL, GT * CP), F32),
            pltpu.VMEM((O * O * BL, CP), F32),
            pltpu.VMEM((O, CP, NF), BF16),
            pltpu.VMEM((O, CP, NF), BF16),
            pltpu.SemaphoreType.DMA((10,)),
        ],
        compiler_params=pltpu.CompilerParams(vmem_limit_bytes=20 << 20),
    )(in_hbm(received), in_hbm(slots), valid, rank, in_hbm(high), in_hbm(low))


def finish_kernel(a_ref, b_ref, pick_ref, keep_ref, divisor_ref, out_ref):
    folded = from_lanes(a_ref[...] + b_ref[...])
    source = iota((J4, J4), 0)
    target = iota((J4, J4), 1)
    move = (source % BL) * O + source // BL == target
    high, low = halves(folded)
    folded = dot(high, one_hot(move)) + dot(low, one_hot(move))
    high, low = halves(jnp.transpose(folded))
    pick = pick_ref[...].astype(BF16)
    wide = dot(high, pick) + dot(low, pick)
    wide = jnp.where(keep_ref[...] > 0, wide, 0.0) / divisor_ref[...]
    out_ref[...] = wide[:, 0:CL]


def finish(a, b, pick, keep, divisor):
    return pl.pallas_call(
        finish_kernel,
        name="finish",
        out_shape=pltpu.HBM((J4, CL), F32),
        compiler_params=pltpu.CompilerParams(vmem_limit_bytes=4 << 20),
    )(a, b, pick, keep, divisor)


def packed_form(amplitudes, cycle_weight, occ_irrep, vir_irrep, occ_energy, vir_energy):
    g = lax.axis_index("grp")
    vir_row = vir_irrep.reshape(1, V)
    sent = pack(occ_irrep, vir_row, amplitudes)
    received = lax.all_to_all(sent, "blk", 0, 0, tiled=True)

    slots, valid, fits, rank, pick, keep, divisor = tables(occ_irrep, vir_irrep, occ_energy, vir_energy)
    own = lax.dynamic_slice_in_dim(jnp.pad(vir_irrep, (0, CP - CL)), g * CL, CP)
    own = jnp.where(jnp.arange(CP) < CL, own, NONE)
    have = jnp.bitwise_xor(own[:, None], occ_irrep[None, :]).reshape(1, CP * O)
    high, low = fold(occ_irrep, vir_row, have, cycle_weight.T)
    fits, slots = lax.optimization_barrier((fits[0, 0] > 0.5, slots))

    partial = contract(received, slots, valid, rank, high, low)
    near = lax.ppermute(partial[1:3], "grp", [(d, d ^ 1) for d in range(G)])
    mine = partial[0] + near[0]
    last = lax.ppermute(partial[3] + near[1], "grp", [(d, d ^ 3) for d in range(G)])
    return finish(mine, last, pick, keep, divisor).T, fits


def plain_form(amplitudes, cycle_weight, occ_irrep, vir_irrep, occ_energy, vir_energy):
    g = lax.axis_index("grp")
    m = lax.axis_index("blk")
    own = lax.dynamic_slice_in_dim(vir_irrep, g * CL, CL)
    own_b = lax.dynamic_slice_in_dim(vir_irrep, m * BL, BL)
    sent = jnp.transpose(amplitudes.reshape(T * CL, BW)).reshape(M, BL, T * CL)
    received = lax.all_to_all(sent, "blk", 0, 0, tiled=True)
    amp = jnp.transpose(received.reshape(M, BL, T, CL), (0, 2, 1, 3)).reshape(O, O, BL, CL)
    pairs = jnp.bitwise_xor(occ_irrep[:, None], occ_irrep[None, :])
    allowed = jnp.bitwise_xor(pairs[:, :, None], own_b)[..., None] == own
    amp = jnp.where(allowed, amp, jnp.zeros_like(amp))
    weight = cycle_weight.reshape(V, CL, O)
    need = jnp.bitwise_xor(vir_irrep, occ_irrep[0])
    have = jnp.bitwise_xor(own[:, None], occ_irrep[None, :])
    weight = jnp.where(need[:, None, None] == have, weight, jnp.zeros_like(weight))
    partial = jnp.einsum("kjbc,xck->xbj", amp, weight, precision=HIGHEST).reshape(G, CL, J4)
    cycle = jnp.sum(lax.all_to_all(partial, "grp", 0, 0, tiled=True).reshape(G, CL, J4), axis=0)
    row_energy = occ_energy[0] - lax.dynamic_slice_in_dim(vir_energy, g * CL, CL)
    slab_energy = lax.dynamic_slice_in_dim(vir_energy, m * BL, BL)
    col_energy = (occ_energy[None, :] - slab_energy[:, None]).reshape(J4)
    return cycle / (row_energy[:, None] + col_energy[None, :])


def shards(*arrays):
    out, fits = packed_form(*arrays)
    return lax.cond(fits, lambda: out, lambda: plain_form(*arrays))


def solution(mesh):
    in_specs = (P("blk", "grp", None), P(None, "grp"), P(), P(), P(), P())
    out_specs = P("grp", "blk")
    return jax.shard_map(shards, mesh=mesh, in_specs=in_specs, out_specs=out_specs, check_vma=False)
```
